128 devices in a mesh: row: 8 (over y, core), col: 16 (over z, x).
Axes of the slice: x: 4, y: 4, z: 4, core: 2. Of those that a mesh axis runs over, the one named last changes fastest.
Arguments:
- near_blocks: bfloat16 [256, 16, 512, 512], P(('row', 'col')), may hold values from -2 to 9, as said below
- leaf_basis: bfloat16 [256, 512, 512], P(('row', 'col')), may hold values from -1 to 2, as said below
- near_cols: int32 [256, 16], P(('row', 'col')), may hold values from 0 to 255, as said below
- near_count: int32 [256], P(('row', 'col')), may hold values from 1 to 16, as said below
- children: int32 [128, 2], replicated, may hold values from 0 to 255, as said below
- parent_basis: bfloat16 [128, 256, 256], P(('row', 'col')), may hold values from -1 to 2, as said below
- far_coupling: float32 [128, 128, 128], P(('row', 'col')), may hold values from -0.25 to 0.25
Outputs:
- leaf_factor: float32 [256, 384, 384], P(('row', 'col'))
- near_schur: float32 [256, 16, 128, 128], P(('row', 'col'))
- top_factor: float32 [128, 128, 128], P(('row', 'col'))
- top_schur: float32 [128, 128, 128], P(('row', 'col'))
The draws below stay inside these ranges and needn't reach their ends.
Inputs may be any that keep to these rules, and one draw needn't show every extreme that they name: near_cols[i, 0] = i; for 1 <= t < near_count[i] the entries near_cols[i, t] are distinct leaves other than i of i's group, the leaves 32 * g to 32 * g + 31 with g = i // 32; slots t >= near_count[i] hold i. `near_count`: some leaf has 16 live slots. Parent p belongs to group g = 2 * p // 32; children[p, 0] is a leaf of group g and children[p, 1] a leaf of group g + 1 - 2 * (g % 2); every leaf is a child of exactly one parent. near_blocks[i, 0] is symmetric positive definite. `leaf_basis`: each basis is nonsingular. `parent_basis`: each basis is nonsingular.
All inputs are finite; a program needn't handle non-finite values.
Results may differ from the reference program's by a relative error of at most 0.0015.
Values may be sent and summed in bfloat16 or wider, within the bound.
No kernel may reach another device: no remote copies, remote signals or barrier semaphores. Data moves between devices by JAX's collectives and lax.ppermute only.
A program may use at most 192 MiB of HBM per device.

```python
import jax
import jax.numpy as jnp
from jax import lax

LEAF = 512
RANK = 128
NB = 16
GROUP = 32
LEAVES = 256
PARENTS = 128


def draw_near_blocks(key, part):
    key_noise = jax.random.fold_in(key, 101)
    key_diag = jax.random.fold_in(key, 102)
    shape = (LEAVES, NB, LEAF, LEAF)
    noise = jnp.clip(jax.random.normal(key_noise, shape, jnp.float32), -5.0, 5.0)
    diag_values = jnp.exp(jax.random.uniform(key_diag, (LEAVES, LEAF), jnp.float32, 1.3863, 2.0794))
    self_noise = noise[:, 0]
    sym_scale = 1.25 / (LEAF ** 0.5 * 1.41421356)
    symmetric = (self_noise + jnp.swapaxes(self_noise, 1, 2)) * sym_scale
    identity = jnp.eye(LEAF, dtype=jnp.float32)
    self_block = symmetric + identity[None] * diag_values[:, None, :] + 0.04
    others = noise[:, 1:] * 0.1
    blocks = jnp.concatenate([self_block[:, None], others], axis=1)
    return blocks.astype(jnp.bfloat16)


def near_identity(key, count, order):
    shape = (count, order, order)
    noise = jnp.clip(jax.random.normal(key, shape, jnp.float32), -5.0, 5.0)
    identity = jnp.eye(order, dtype=jnp.float32)
    return (identity[None] + noise * (0.2 / order ** 0.5)).astype(jnp.bfloat16)


def draw_leaf_basis(key, part):
    return near_identity(jax.random.fold_in(key, 201), LEAVES, LEAF)


def draw_parent_basis(key, part):
    return near_identity(jax.random.fold_in(key, 202), PARENTS, 2 * RANK)


def count_draw(key):
    key_counts = jax.random.fold_in(key, 7)
    key_pick = jax.random.fold_in(key, 8)
    light_most = max(3, NB // 3)
    counts = jax.random.randint(key_counts, (LEAVES,), 1, light_most + 1)
    chosen = jax.random.randint(key_pick, (), 0, LEAVES)
    counts = jnp.where(jnp.arange(LEAVES) == chosen, NB, counts)
    return counts.astype(jnp.int32)


def draw_near_count(key, part):
    return count_draw(key)


def draw_near_cols(key, part):
    counts = count_draw(key)
    key_scores = jax.random.fold_in(key, 13)
    positions = jnp.arange(GROUP, dtype=jnp.int32)
    leaf_ids = jnp.arange(LEAVES, dtype=jnp.int32)
    scores = jax.random.randint(key_scores, (LEAVES, GROUP), 0, 1 << 20) * GROUP + positions[None]
    own_offset = leaf_ids % GROUP
    scores = jnp.where(positions[None] == own_offset[:, None], -1, scores)
    order = jnp.argsort(scores, axis=1, stable=True)[:, :NB]
    columns = (leaf_ids // GROUP * GROUP)[:, None] + order
    slot_ids = jnp.arange(NB, dtype=jnp.int32)
    columns = jnp.where(slot_ids[None] < counts[:, None], columns, leaf_ids[:, None])
    return columns.astype(jnp.int32)


def draw_children(key, part):
    key_perm = jax.random.fold_in(key, 17)
    groups = LEAVES // GROUP
    half = GROUP // 2

    def one_perm(sub_key):
        return jax.random.permutation(sub_key, GROUP)
    perms = jax.vmap(one_perm)(jax.random.split(key_perm, groups))
    group_ids = jnp.arange(groups, dtype=jnp.int32)
    partner = group_ids + 1 - 2 * (group_ids % 2)
    first_kid = group_ids[:, None] * GROUP + perms[:, :half]
    second_kid = partner[:, None] * GROUP + perms[partner][:, half:]
    return jnp.stack([first_kid.reshape(-1), second_kid.reshape(-1)], axis=1).astype(jnp.int32)


def block_scale(own_key, dims, cuts, low, top_value):
    def one(position, shards_of):
        heights = jax.random.uniform(jax.random.fold_in(jax.random.fold_in(own_key, 6), position), (shards_of,), jnp.float32, low / len(cuts), top_value / len(cuts))
        return jnp.repeat(jnp.exp(heights), dims[position] // shards_of).reshape((-1,) + (1,) * (len(dims) - position - 1))

    factor_of = one(*cuts[0])
    for cut in cuts[1:]:
        factor_of = factor_of * one(*cut)
    return factor_of


def scatter_about(own_key, dims, scale, bound, pieces=(), kind=jnp.bfloat16):
    drawn = scale * jax.random.normal(own_key, dims, jnp.float32)
    if pieces:
        drawn = drawn * block_scale(own_key, dims, pieces, -0.22, 0.18)
    return jnp.clip(drawn, -bound, bound).astype(kind)


def setup_inputs(seed: int = 0) -> dict:
    streams_of = jax.random.split(jax.random.key(seed), 8)
    return {
        "near_blocks": draw_near_blocks(jax.random.fold_in(streams_of[7], 71), 0),
        "leaf_basis": draw_leaf_basis(jax.random.fold_in(streams_of[7], 71), 0),
        "near_cols": draw_near_cols(jax.random.fold_in(streams_of[7], 71), 0),
        "near_count": draw_near_count(jax.random.fold_in(streams_of[7], 71), 0),
        "children": draw_children(jax.random.fold_in(streams_of[7], 71), 0),
        "parent_basis": draw_parent_basis(jax.random.fold_in(streams_of[7], 71), 0),
        "far_coupling": scatter_about(streams_of[6], (PARENTS, RANK, RANK), (0.2 / RANK ** 0.5), 0.25, ((0, 128),), jnp.float32),
    }


HIGHEST = lax.Precision.HIGHEST

def rotate_pivot(near_block, basis):
    red_size = LEAF - RANK
    product = jnp.dot(near_block.astype(jnp.float32), basis.astype(jnp.float32), preferred_element_type=jnp.float32)
    rotated = jnp.dot(basis.astype(jnp.float32).T, product, precision=HIGHEST)
    factor = jnp.linalg.cholesky(rotated[:red_size, :red_size])
    pivot = jax.scipy.linalg.cho_solve((factor, True), rotated[:red_size, red_size:])
    self_schur = rotated[red_size:, red_size:] - jnp.dot(rotated[red_size:, :red_size], pivot, precision=HIGHEST)
    return (factor, pivot, self_schur)

def pair_schur(near_block, basis_own, pivot_own, basis_other, pivot_other):
    red_size = LEAF - RANK
    product = jnp.dot(near_block.astype(jnp.float32), basis_other.astype(jnp.float32), preferred_element_type=jnp.float32)
    own_float = basis_own.astype(jnp.float32)
    skel_rows = jnp.dot(own_float[:, red_size:].T, product, precision=HIGHEST)
    red_rows = jnp.dot(own_float[:, :red_size].T, product[:, red_size:], precision=HIGHEST)
    return skel_rows[:, red_size:] - jnp.dot(skel_rows[:, :red_size], pivot_other, precision=HIGHEST) - jnp.dot(pivot_own.T, red_rows, precision=HIGHEST)

def reference(near_blocks, leaf_basis, near_cols, near_count, children, parent_basis, far_coupling):

    def diag_part(pair_args):
        return rotate_pivot(pair_args[0], pair_args[1])
    factors, pivots, diag_schur = lax.map(diag_part, (near_blocks[:, 0], leaf_basis))
    slot_ids = jnp.arange(NB, dtype=jnp.int32)

    def leaf_row(row_args):
        blocks, leaf_id, columns, count = row_args

        def slot_term(slot_args):
            near_block, column = slot_args
            return pair_schur(near_block, leaf_basis[leaf_id], pivots[leaf_id], leaf_basis[column], pivots[column])
        terms = lax.map(slot_term, (blocks[1:], columns[1:]))
        schur_rows = jnp.concatenate([diag_schur[leaf_id][None], terms], axis=0)
        live = slot_ids < count
        return jnp.where(live[:, None, None], schur_rows, jnp.float32(0.0))
    near_schur = lax.map(leaf_row, (near_blocks, jnp.arange(LEAVES, dtype=jnp.int32), near_cols, near_count))

    def parent_part(parent_args):
        kids, basis, coupling = parent_args
        first_block = diag_schur[kids[0]]
        second_block = diag_schur[kids[1]]
        upper = jnp.concatenate([first_block, coupling], axis=1)
        lower = jnp.concatenate([coupling.T, second_block], axis=1)
        merged = jnp.concatenate([upper, lower], axis=0)
        basis_float = basis.astype(jnp.float32)
        rotated = jnp.dot(basis_float.T, jnp.dot(merged, basis_float, precision=HIGHEST), precision=HIGHEST)
        factor = jnp.linalg.cholesky(rotated[:RANK, :RANK])
        solved = jax.scipy.linalg.cho_solve((factor, True), rotated[:RANK, RANK:])
        top = rotated[RANK:, RANK:] - jnp.dot(rotated[RANK:, :RANK], solved, precision=HIGHEST)
        return (factor, top)
    top_factor, top_schur = lax.map(parent_part, (children, parent_basis, far_coupling))
    return (factors, near_schur, top_factor, top_schur)
```

```python
from functools import partial

import jax
import jax.numpy as jnp
from jax import lax
from jax.experimental import pallas as pl
from jax.experimental.pallas import tpu as pltpu
from jax.sharding import PartitionSpec as P

F32 = jnp.float32
BF16 = jnp.bfloat16
LANE = 128
SUB = 8
VMEM_BYTES = 56 << 20


def split2(x):
    hi = x.astype(BF16)
    lo = (x - hi.astype(F32)).astype(BF16)
    return hi, lo


def dot(a, b):
    return jnp.dot(a, b, preferred_element_type=F32)


def dot_first(a, b):
    return lax.dot_general(a, b, (((0,), (0,)), ((), ())), preferred_element_type=F32)


def mul3(a, b, op=dot):
    ah, al = split2(a)
    bh, bl = split2(b)
    return op(ah, bh) + (op(ah, bl) + op(al, bh))


def lower_inverse(work, inv):
    n = LANE
    row = lax.broadcasted_iota(jnp.int32, (n, n), 0)
    col = lax.broadcasted_iota(jnp.int32, (n, n), 1)
    eye = jnp.where(row == col, 1.0, 0.0).astype(F32)
    sub = lax.broadcasted_iota(jnp.int32, (SUB, n), 0)
    for t in inv:
        t[...] = eye
    for k in range(0, n, SUB):
        panels = []
        for a, t in zip(work, inv):
            pa = a[k : k + SUB, :]
            pt = t[k : k + SUB, :]
            cols = [jnp.broadcast_to(pa[:, k + j : k + j + 1], (SUB, n)) for j in range(SUB)]
            panels.append([pa, pt, cols])
        for j in range(SUB):
            for panel in panels:
                pa, pt, cols = panel
                d = jnp.broadcast_to(cols[j][j : j + 1, :], (SUB, n))
                r = lax.rsqrt(d)
                c = cols[j] * r
                ra = jnp.broadcast_to(pa[j : j + 1, :], (SUB, n)) * r
                rt = jnp.broadcast_to(pt[j : j + 1, :], (SUB, n)) * r
                cm = jnp.where(sub > j, c, 0.0)
                panel[0] = jnp.where(sub == j, ra, pa - cm * ra)
                panel[1] = jnp.where(sub == j, rt, pt - cm * rt)
                for m in range(j + 1, SUB):
                    cols[m] = cols[m] - c * jnp.broadcast_to(c[m : m + 1, :], (SUB, n))
        for (pa, pt, _), a, t in zip(panels, work, inv):
            a[k : k + SUB, :] = pa
            t[k : k + SUB, :] = pt
            if k + SUB < n:
                both = jnp.concatenate([pa, pt], axis=1)
                hi = both.astype(BF16).astype(F32)
                lo = both - hi
                left = jnp.concatenate([hi[:, :n], hi[:, :n], lo[:, :n], lo[:, :n]], axis=0).astype(BF16)
                right = jnp.concatenate([hi, lo, hi, lo], axis=0).astype(BF16)
                upd = dot_first(left, right)
                a[k + SUB :, :] = a[k + SUB :, :] - upd[k + SUB :, :n]
                t[k + SUB :, :] = t[k + SUB :, :] - upd[k + SUB :, n:]


def diag_kernel(a_ref, u_ref, factor_ref, q_ref, schur_ref, w_ref, t_ref):
    leaves = u_ref.shape[0]
    size = u_ref.shape[1]
    n = LANE
    blocks = size // n - 1
    red = blocks * n
    row = lax.broadcasted_iota(jnp.int32, (n, n), 0)
    col = lax.broadcasted_iota(jnp.int32, (n, n), 1)
    upper = row <= col
    for i in range(leaves):
        u = u_ref[i]
        hh, hl = split2(dot(a_ref[i, 0], u))
        w_ref[i] = dot_first(u, hh) + dot_first(u, hl)
    for b in range(blocks):
        lo, hi = b * n, (b + 1) * n
        lower_inverse(
            [w_ref.at[i, lo:hi, lo:hi] for i in range(leaves)],
            [t_ref.at[i, b] for i in range(leaves)],
        )
        for i in range(leaves):
            x = mul3(t_ref[i, b], w_ref[i, lo:hi, hi:])
            w_ref[i, lo:hi, hi:] = x
            xh, xl = split2(x)
            w_ref[i, hi:, hi:] = w_ref[i, hi:, hi:] - (
                dot_first(xh, xh) + (dot_first(xh, xl) + dot_first(xl, xh))
            )
    for i in range(leaves):
        schur_ref[i] = w_ref[i, red:, red:]
        piv = [None] * blocks
        for b in reversed(range(blocks)):
            lo, hi = b * n, (b + 1) * n
            y = w_ref[i, lo:hi, red:]
            if b + 1 < blocks:
                y = y - mul3(w_ref[i, lo:hi, hi:red], jnp.concatenate(piv[b + 1 :], axis=0))
            piv[b] = mul3(t_ref[i, b], y, dot_first)
        ph, plo = split2(jnp.concatenate(piv, axis=0))
        ur = u_ref[i, :, :red]
        q_ref[i] = (dot(ur, ph) + dot(ur, plo)).astype(BF16)
        for b in range(blocks):
            for c in range(blocks):
                if c < b:
                    blk = w_ref[i, c * n : (c + 1) * n, b * n : (b + 1) * n].T
                elif c == b:
                    blk = jnp.where(upper, w_ref[i, b * n : (b + 1) * n, b * n : (b + 1) * n], 0.0).T
                else:
                    blk = jnp.zeros((n, n), F32)
                factor_ref[i, b * n : (b + 1) * n, c * n : (c + 1) * n] = blk


def diag_part(near_blocks, leaf_basis):
    leaves, size, _ = leaf_basis.shape
    red = size - LANE
    return pl.pallas_call(
        diag_kernel,
        grid=(1,),
        in_specs=[
            pl.BlockSpec((leaves, 1, size, size), lambda g: (0, 0, 0, 0)),
            pl.BlockSpec((leaves, size, size), lambda g: (0, 0, 0)),
        ],
        out_specs=[
            pl.BlockSpec((leaves, red, red), lambda g: (0, 0, 0)),
            pl.BlockSpec((leaves, size, LANE), lambda g: (0, 0, 0)),
            pl.BlockSpec((leaves, LANE, LANE), lambda g: (0, 0, 0)),
        ],
        out_shape=[
            jax.ShapeDtypeStruct((leaves, red, red), F32),
            jax.ShapeDtypeStruct((leaves, size, LANE), BF16),
            jax.ShapeDtypeStruct((leaves, LANE, LANE), F32),
        ],
        scratch_shapes=[
            pltpu.VMEM((leaves, size, size), F32),
            pltpu.VMEM((leaves, size // LANE - 1, LANE, LANE), F32),
        ],
        compiler_params=pltpu.CompilerParams(vmem_limit_bytes=VMEM_BYTES),
        name="diag",
    )(near_blocks, leaf_basis)


def near_kernel(off_ref, cnt_ref, a_hbm, s_ref, q_ref, schur_ref, sg_ref, qg_ref, out_ref, a_buf, left_ref, sem):
    leaves, slots = out_ref.shape[:2]

    def copy(i, t):
        return pltpu.make_async_copy(a_hbm.at[i, t], a_buf.at[i, t - 1], sem.at[i, t - 1])

    for i in range(leaves):
        lax.fori_loop(1, cnt_ref[i], lambda t, _, i=i: copy(i, t).start(), None)
    for i in range(leaves):
        left_ref[:LANE, :] = s_ref[i].T
        left_ref[LANE:, :] = q_ref[i].T
        out_ref[i, 0] = schur_ref[i]

        def live(t, _, i=i):
            copy(i, t).wait()
            j = off_ref[i * slots + t]
            g = dot(left_ref[...], a_buf[i, t - 1])
            g_s = g[:LANE]
            gh, gl = split2(g_s - g[LANE:])
            s_j = sg_ref[j]
            out_ref[i, t] = (dot(gh, s_j) + dot(gl, s_j)) - dot(g_s.astype(BF16), qg_ref[j])

        def dead(t, _, i=i):
            out_ref[i, t] = jnp.zeros(out_ref.shape[2:], F32)

        lax.fori_loop(1, cnt_ref[i], live, None)
        lax.fori_loop(cnt_ref[i], slots, dead, None)


def near_part(offsets, counts, near_blocks, own_s, own_q, schur, s_all, q_all):
    leaves, slots, size, _ = near_blocks.shape
    vmem = pl.BlockSpec(memory_space=pltpu.VMEM)
    smem = pl.BlockSpec(memory_space=pltpu.SMEM)
    return pl.pallas_call(
        near_kernel,
        in_specs=[smem, smem, pl.BlockSpec(memory_space=pl.ANY), vmem, vmem, vmem, vmem, vmem],
        out_specs=vmem,
        out_shape=jax.ShapeDtypeStruct((leaves, slots, LANE, LANE), F32),
        scratch_shapes=[
            pltpu.VMEM((leaves, slots - 1, size, size), BF16),
            pltpu.VMEM((2 * LANE, size), BF16),
            pltpu.SemaphoreType.DMA((leaves, slots - 1)),
        ],
        compiler_params=pltpu.CompilerParams(vmem_limit_bytes=VMEM_BYTES),
        name="near",
    )(offsets, counts, near_blocks, own_s, own_q, schur, s_all, q_all)


def top_kernel(first_ref, second_ref, far_ref, v_ref, factor_ref, top_ref, w_ref, t_ref):
    n = LANE
    row = lax.broadcasted_iota(jnp.int32, (n, n), 0)
    col = lax.broadcasted_iota(jnp.int32, (n, n), 1)
    far = far_ref[0]
    merged = jnp.concatenate(
        [jnp.concatenate([first_ref[...], far], axis=1), jnp.concatenate([far.T, second_ref[...]], axis=1)], axis=0
    )
    v = v_ref[0]
    mh, ml = split2(merged)
    hh, hl = split2(dot(mh, v) + dot(ml, v))
    p = dot_first(v, hh) + dot_first(v, hl)
    w_ref[...] = p[:n, :n]
    lower_inverse([w_ref], [t_ref])
    x = mul3(t_ref[...], p[:n, n:])
    top_ref[0] = p[n:, n:] - mul3(x, x, dot_first)
    factor_ref[0] = jnp.where(row <= col, w_ref[...], 0.0).T


def top_part(first, second, far, basis):
    shape = jax.ShapeDtypeStruct((1, LANE, LANE), F32)
    return pl.pallas_call(
        top_kernel,
        out_shape=[shape, shape],
        scratch_shapes=[pltpu.VMEM((LANE, LANE), F32), pltpu.VMEM((LANE, LANE), F32)],
        compiler_params=pltpu.CompilerParams(vmem_limit_bytes=VMEM_BYTES),
        name="top",
    )(first, second, far, basis)


def local(near_blocks, leaf_basis, near_cols, near_count, children, parent_basis, far_coupling):
    leaves, slots = near_cols.shape
    size = leaf_basis.shape[1]
    red = size - LANE
    row_index = lax.axis_index("row")
    col_index = lax.axis_index("col")
    row_count = lax.axis_size("row")
    col_count = lax.axis_size("col")
    group_size = leaves * col_count
    group_base = row_index * group_size
    own_s = leaf_basis[:, :, red:]
    s_all = lax.all_gather(own_s, "col", axis=0, tiled=True)
    factors, own_q, schur = diag_part(near_blocks, leaf_basis)
    schur_all = lax.all_gather(schur, "col", axis=0, tiled=True)
    q_all = lax.all_gather(own_q, "col", axis=0, tiled=True)
    partner_row = row_index + 1 - 2 * (row_index % 2)
    parent_id = row_index * col_count + col_index
    partner_parent = partner_row * col_count + col_index
    first = schur_all[children[parent_id, 0] - group_base]
    outgoing = schur_all[children[partner_parent, 1] - group_base]
    second = lax.ppermute(outgoing, "row", [(r, r ^ 1) for r in range(row_count)])
    top_factor, top_schur = top_part(first, second, far_coupling, parent_basis)
    offsets = (near_cols - group_base).reshape(-1)
    near_schur = near_part(offsets, near_count, near_blocks, own_s, own_q, schur, s_all, q_all)
    return factors, near_schur, top_factor, top_schur


def solution(mesh):
    both = ("row", "col")
    return jax.shard_map(
        local,
        mesh=mesh,
        in_specs=(P(both), P(both), P(both), P(both), P(), P(both), P(both)),
        out_specs=(P(both), P(both), P(both), P(both)),
        check_vma=False,
    )
```

```python
from functools import partial

import jax
import jax.numpy as jnp
from jax import lax
from jax.experimental import pallas as pl
from jax.experimental.pallas import tpu as pltpu
from jax.sharding import PartitionSpec as P

F32 = jnp.float32
BF16 = jnp.bfloat16
LANE = 128
SUB = 8
HBM = pl.BlockSpec(memory_space=pltpu.HBM)
VMEM = pl.BlockSpec(memory_space=pltpu.VMEM)
SMEM = pl.BlockSpec(memory_space=pltpu.SMEM)
LARGE = pltpu.CompilerParams(vmem_limit_bytes=60 << 20)
STEP = 4


def guess(us):
    return pl.CostEstimate(flops=int(us * 1e9), bytes_accessed=0, transcendentals=0)


def split2(x):
    hi = x.astype(BF16)
    lo = (x - hi.astype(F32)).astype(BF16)
    return hi, lo


def dot(a, b):
    return jnp.dot(a, b, preferred_element_type=F32)


def dot_first(a, b):
    return lax.dot_general(a, b, (((0,), (0,)), ((), ())), preferred_element_type=F32)


def mul3(a, b, op=dot):
    ah, al = split2(a)
    bh, bl = split2(b)
    return op(ah, bh) + (op(ah, bl) + op(al, bh))


def spread(row):
    return jnp.broadcast_to(row, (SUB, row.shape[1]))


def lower_inverse(work, inv):
    n = LANE
    groups = 2
    width = groups * SUB
    row = lax.broadcasted_iota(jnp.int32, (n, n), 0)
    col = lax.broadcasted_iota(jnp.int32, (n, n), 1)
    eye = jnp.where(row == col, 1.0, 0.0).astype(F32)
    sub = lax.broadcasted_iota(jnp.int32, (SUB, n), 0)
    for t in inv:
        t[...] = eye
    for k in range(0, n, width):
        panels = []
        for a, t in zip(work, inv):
            pa = [a[k + g * SUB : k + (g + 1) * SUB, :] for g in range(groups)]
            pt = [t[k + g * SUB : k + (g + 1) * SUB, :] for g in range(groups)]
            cols = [
                [jnp.broadcast_to(pa[g][:, k + j : k + j + 1], (SUB, n)) for j in range((g + 1) * SUB)]
                for g in range(groups)
            ]
            panels.append((pa, pt, cols))
        for j in range(width):
            own, jj = divmod(j, SUB)
            for pa, pt, cols in panels:
                r = lax.rsqrt(spread(cols[own][j][jj : jj + 1]))
                r2 = r * r
                ra = spread(pa[own][jj : jj + 1]) * r
                rt = spread(pt[own][jj : jj + 1]) * r
                elems = {}
                for g in range(own, groups):
                    for m in range(max(j + 1, g * SUB), (g + 1) * SUB):
                        elems[m] = spread(cols[g][j][m - g * SUB : m - g * SUB + 1])
                for g in range(own, groups):
                    base = cols[g][j]
                    for m in range(j + 1, (g + 1) * SUB):
                        cols[g][m] = cols[g][m] - (base * elems[m]) * r2
                    c = base * r
                    if g == own:
                        c = jnp.where(sub > jj, c, 0.0)
                        pa[g] = jnp.where(sub == jj, ra, pa[g] - c * ra)
                        pt[g] = jnp.where(sub == jj, rt, pt[g] - c * rt)
                    else:
                        pa[g] = pa[g] - c * ra
                        pt[g] = pt[g] - c * rt
        for (pa, pt, _), a, t in zip(panels, work, inv):
            a_rows = jnp.concatenate(pa, axis=0)
            t_rows = jnp.concatenate(pt, axis=0)
            a[k : k + width, :] = a_rows
            t[k : k + width, :] = t_rows
            if k + width < n:
                hi, lo = split2(jnp.concatenate([a_rows, t_rows], axis=1))
                left = jnp.concatenate([hi[:, :n], hi[:, :n], lo[:, :n], lo[:, :n]], axis=0)
                right = jnp.concatenate([hi, lo, hi, lo], axis=0)
                upd = dot_first(left, right)
                a[k + width :, :] = a[k + width :, :] - upd[k + width :, :n]
                t[k + width :, :] = t[k + width :, :] - upd[k + width :, n:]


def pack_symmetric(m):
    n = LANE
    row = lax.broadcasted_iota(jnp.int32, (n, n), 0)
    col = lax.broadcasted_iota(jnp.int32, (n, n), 1)
    m = jnp.where(row >= col, m, m.T)
    hi = m.astype(BF16).astype(F32)
    lo = m - hi
    last = jnp.sum(jnp.where(row == col, lo, 0.0), axis=0, keepdims=True)
    body = jnp.where(row >= col, hi, lo)
    return jnp.concatenate([body, jnp.broadcast_to(last, (16, n))], axis=0).astype(BF16)


def unpack_symmetric(packed):
    n = LANE
    row = lax.broadcasted_iota(jnp.int32, (n, n), 0)
    col = lax.broadcasted_iota(jnp.int32, (n, n), 1)
    packed = packed.astype(F32)
    body = packed[:n]
    other = body.T
    last = jnp.broadcast_to(packed[n : n + 1], (n, n))
    return jnp.where(row == col, body + last, body + other)


def diag_kernel(a_ref, u_ref, factor_ref, pay_ref, schur_ref, w_ref, t_ref):
    leaves = u_ref.shape[0]
    size = u_ref.shape[1]
    n = LANE
    blocks = size // n - 1
    red = blocks * n
    row = lax.broadcasted_iota(jnp.int32, (n, n), 0)
    col = lax.broadcasted_iota(jnp.int32, (n, n), 1)
    upper = row <= col
    for i in range(leaves):
        u = u_ref[i]
        hh, hl = split2(dot(a_ref[i, 0], u))
        w_ref[i] = dot_first(u, hh) + dot_first(u, hl)
    for b in range(blocks):
        lo, hi = b * n, (b + 1) * n
        lower_inverse(
            [w_ref.at[i, lo:hi, lo:hi] for i in range(leaves)],
            [t_ref.at[i, b] for i in range(leaves)],
        )
        for i in range(leaves):
            x = mul3(t_ref[i, b], w_ref[i, lo:hi, hi:])
            w_ref[i, lo:hi, hi:] = x
            xh, xl = split2(x)
            w_ref[i, hi:, hi:] = w_ref[i, hi:, hi:] - (
                dot_first(xh, xh) + (dot_first(xh, xl) + dot_first(xl, xh))
            )
    for i in range(leaves):
        schur = w_ref[i, red:, red:]
        schur_ref[i] = schur
        pay_ref[i, :size, :] = u_ref[i, :, red:]
        pay_ref[i, 2 * size :, :] = pack_symmetric(schur)
        piv = [None] * blocks
        for b in reversed(range(blocks)):
            lo, hi = b * n, (b + 1) * n
            y = w_ref[i, lo:hi, red:]
            if b + 1 < blocks:
                y = y - mul3(w_ref[i, lo:hi, hi:red], jnp.concatenate(piv[b + 1 :], axis=0))
            piv[b] = mul3(t_ref[i, b], y, dot_first)
        ph, plo = split2(jnp.concatenate(piv, axis=0))
        ur = u_ref[i, :, :red]
        pay_ref[i, size : 2 * size, :] = (dot(ur, ph) + dot(ur, plo)).astype(BF16)
        for b in range(blocks):
            for c in range(blocks):
                if c < b:
                    blk = w_ref[i, c * n : (c + 1) * n, b * n : (b + 1) * n].T
                elif c == b:
                    blk = jnp.where(upper, w_ref[i, b * n : (b + 1) * n, b * n : (b + 1) * n], 0.0).T
                else:
                    blk = jnp.zeros((n, n), F32)
                factor_ref[i, b * n : (b + 1) * n, c * n : (c + 1) * n] = blk


def diag_part(near_blocks, leaf_basis):
    leaves, size, _ = leaf_basis.shape
    red = size - LANE
    rows = 2 * size + LANE + 16
    return pl.pallas_call(
        diag_kernel,
        grid=(1,),
        in_specs=[
            pl.BlockSpec((leaves, 1, size, size), lambda g: (0, 0, 0, 0)),
            pl.BlockSpec((leaves, size, size), lambda g: (0, 0, 0)),
        ],
        out_specs=[
            pl.BlockSpec((leaves, red, red), lambda g: (0, 0, 0)),
            pl.BlockSpec((leaves, rows, LANE), lambda g: (0, 0, 0)),
            pl.BlockSpec((leaves, LANE, LANE), lambda g: (0, 0, 0)),
        ],
        out_shape=[
            jax.ShapeDtypeStruct((leaves, red, red), F32),
            jax.ShapeDtypeStruct((leaves, rows, LANE), BF16),
            jax.ShapeDtypeStruct((leaves, LANE, LANE), F32),
        ],
        scratch_shapes=[
            pltpu.VMEM((leaves, size, size), F32),
            pltpu.VMEM((leaves, size // LANE - 1, LANE, LANE), F32),
        ],
        compiler_params=LARGE,
        cost_estimate=guess(26),
        name="diag",
    )(near_blocks, leaf_basis)


def pick_kernel(where_ref, *refs):
    pieces, (first_ref, second_ref, sem) = refs[:-3], refs[-3:]
    rows = first_ref.shape[0]
    half = len(pieces) // 2
    for out, dst in enumerate((first_ref, second_ref)):
        base = 0
        for p, piece in enumerate(pieces):
            if p == half:
                base = 0
            count = piece.shape[0]
            leaf = 0 if p < half else 1
            slot = where_ref[2 * out + 1] - base

            @pl.when((where_ref[2 * out] == leaf) & (slot >= 0) & (slot < count))
            def _(piece=piece, slot=slot, dst=dst, out=out):
                at = jnp.clip(slot, 0, piece.shape[0] - 1)
                pltpu.make_async_copy(piece.at[at, pl.ds(piece.shape[1] - rows, rows)], dst, sem.at[out]).start()

            base += count
    for out, dst in enumerate((first_ref, second_ref)):
        pltpu.make_async_copy(pieces[0].at[0, pl.ds(pieces[0].shape[1] - rows, rows)], dst, sem.at[out]).wait()


def pick_part(where, pieces):
    rows = LANE + 16
    shape = jax.ShapeDtypeStruct((rows, LANE), BF16)
    return pl.pallas_call(
        pick_kernel,
        in_specs=[SMEM] + [HBM] * len(pieces),
        out_shape=[shape, shape],
        scratch_shapes=[pltpu.SemaphoreType.DMA((2,))],
        name="pick",
    )(where, *pieces)


def own_kernel(cnt_ref, a_hbm, pay_ref, g_hbm, a_buf, g_buf, left_ref, a_sem, g_sem):
    leaves, slots, size, _ = a_hbm.shape

    def load(i, t):
        return pltpu.make_async_copy(a_hbm.at[i, t], a_buf.at[i, t], a_sem.at[i, t])

    def save(i, t):
        return pltpu.make_async_copy(g_buf.at[i, t], g_hbm.at[i, t], g_sem.at[i, t])

    for i in range(leaves):
        lax.fori_loop(1, cnt_ref[i], lambda t, _, i=i: load(i, t).start(), None)
    for i in range(leaves):
        left_ref[i, :LANE, :] = pay_ref[i, :size].T
        left_ref[i, LANE:, :] = pay_ref[i, size : 2 * size].T
    for i in range(leaves):

        def some(c, _, i=i):
            for t in [c * STEP + u for u in range(STEP)]:

                @pl.when((t > 0) & (t < cnt_ref[i]))
                def _(t=t):
                    load(i, t).wait()

            for t in [c * STEP + u for u in range(STEP)]:
                g = dot(left_ref[i], a_buf[i, t])
                g_s = g[:LANE]
                hi, lo = split2(g_s - g[LANE:])
                g_buf[i, t, 0] = hi
                g_buf[i, t, 1] = lo
                g_buf[i, t, 2] = g_s.astype(BF16)
            for t in [c * STEP + u for u in range(STEP)]:

                @pl.when((t > 0) & (t < cnt_ref[i]))
                def _(t=t):
                    save(i, t).start()

        lax.fori_loop(0, (cnt_ref[i] + (STEP - 1)) // STEP, some, None)
    for i in range(leaves):
        lax.fori_loop(1, cnt_ref[i], lambda t, _, i=i: save(i, t).wait(), None)


def own_part(counts, near_blocks, pay):
    leaves, slots, size, _ = near_blocks.shape
    shape = (leaves, slots, 3, LANE, size)
    return pl.pallas_call(
        own_kernel,
        in_specs=[SMEM, HBM, VMEM],
        out_specs=HBM,
        out_shape=jax.ShapeDtypeStruct(shape, BF16),
        scratch_shapes=[
            pltpu.VMEM(near_blocks.shape, BF16),
            pltpu.VMEM(shape, BF16),
            pltpu.VMEM((leaves, 2 * LANE, size), BF16),
            pltpu.SemaphoreType.DMA((leaves, slots)),
            pltpu.SemaphoreType.DMA((leaves, slots)),
        ],
        compiler_params=LARGE,
        cost_estimate=guess(8),
        name="own",
    )(counts, near_blocks, pay)


def near_kernel(off_ref, spot_ref, cnt_ref, schur_ref, g_hbm, *refs):
    pieces, (out_ref, g_buf, r_buf, g_sem, r_sem) = refs[:-5], refs[-5:]
    leaves, slots = out_ref.shape[:2]
    rows = r_buf.shape[2]
    half = len(pieces) // 2
    count = pieces[0].shape[0]

    def load(i, t):
        return pltpu.make_async_copy(g_hbm.at[i, t], g_buf.at[i, t], g_sem.at[i, t])

    def fetch(i, t, piece, at):
        return pltpu.make_async_copy(piece.at[at, pl.ds(0, rows)], r_buf.at[i, t], r_sem.at[i, t])

    for i in range(leaves):

        def begin(t, _, i=i):
            load(i, t).start()
            at = i * slots + t
            spot = spot_ref[at]
            number = lax.rem(off_ref[at], 2) * half + lax.div(spot, count)
            for p, piece in enumerate(pieces):

                @pl.when(number == p)
                def _(piece=piece):
                    fetch(i, t, piece, lax.rem(spot, count)).start()

        lax.fori_loop(1, cnt_ref[i], begin, None)
    size = rows // 2
    for i in range(leaves):

        def some(c, _, i=i):
            for t in [c * STEP + u for u in range(STEP)]:

                @pl.when((t > 0) & (t < cnt_ref[i]))
                def _(t=t):
                    load(i, t).wait()
                    fetch(i, t, pieces[0], 0).wait()

            for t in [c * STEP + u for u in range(STEP)]:
                s_j = r_buf[i, t, :size]
                value = dot(g_buf[i, t, 0], s_j) + dot(g_buf[i, t, 1], s_j)
                value = value - dot(g_buf[i, t, 2], r_buf[i, t, size:])
                out_ref[i, t] = jnp.where(t < cnt_ref[i], value, 0.0)

        def dead(t, _, i=i):
            out_ref[i, t] = jnp.zeros(out_ref.shape[2:], F32)

        steps = (cnt_ref[i] + (STEP - 1)) // STEP
        lax.fori_loop(0, steps, some, None)
        lax.fori_loop(steps * STEP, slots, dead, None)
        out_ref[i, 0] = schur_ref[i]


def near_part(offsets, spots, counts, schur, g, pieces):
    leaves, slots, _, _, size = g.shape
    return pl.pallas_call(
        near_kernel,
        in_specs=[SMEM, SMEM, SMEM, VMEM, HBM] + [HBM] * len(pieces),
        out_specs=VMEM,
        out_shape=jax.ShapeDtypeStruct((leaves, slots, LANE, LANE), F32),
        scratch_shapes=[
            pltpu.VMEM(g.shape, BF16),
            pltpu.VMEM((leaves, slots, 2 * size, LANE), BF16),
            pltpu.SemaphoreType.DMA((leaves, slots)),
            pltpu.SemaphoreType.DMA((leaves, slots)),
        ],
        compiler_params=LARGE,
        cost_estimate=guess(6),
        name="near",
    )(offsets, spots, counts, schur, g, *pieces)


def top_kernel(first_ref, second_ref, far_ref, v_ref, factor_ref, top_ref, w_ref, t_ref):
    n = LANE
    row = lax.broadcasted_iota(jnp.int32, (n, n), 0)
    col = lax.broadcasted_iota(jnp.int32, (n, n), 1)
    far = far_ref[0]
    merged = jnp.concatenate(
        [
            jnp.concatenate([unpack_symmetric(first_ref[...]), far], axis=1),
            jnp.concatenate([far.T, unpack_symmetric(second_ref[...])], axis=1),
        ],
        axis=0,
    )
    v = v_ref[0]
    mh, ml = split2(merged)
    hh, hl = split2(dot(mh, v) + dot(ml, v))
    p = dot_first(v, hh) + dot_first(v, hl)
    w_ref[...] = p[:n, :n]
    lower_inverse([w_ref], [t_ref])
    x = mul3(t_ref[...], p[:n, n:])
    top_ref[0] = p[n:, n:] - mul3(x, x, dot_first)
    factor_ref[0] = jnp.where(row <= col, w_ref[...], 0.0).T


def top_part(first, second, far, basis):
    shape = jax.ShapeDtypeStruct((1, LANE, LANE), F32)
    return pl.pallas_call(
        top_kernel,
        out_shape=[shape, shape],
        scratch_shapes=[pltpu.VMEM((LANE, LANE), F32), pltpu.VMEM((LANE, LANE), F32)],
        compiler_params=LARGE,
        cost_estimate=guess(8),
        name="top",
    )(first, second, far, basis)


def shifted(x, side, step_z, step_x):
    route = []
    for i in range(side * side):
        z, w = divmod(i, side)
        route.append((i, (z + step_z) % side * side + (w + step_x) % side))
    return lax.ppermute(x, "col", route)


def ways(side):
    def along_x(v, d):
        return shifted(v, side, 0, d)

    def along_z(v, d):
        return shifted(v, side, d, 0)

    return along_x, along_z


def near_ring(x, shift):
    return shift(x, 1), shift(x, -1)


def close_ring(x, back, ahead, shift):
    cut = (x.shape[0] // 32 + 1) // 2 * 32
    head, tail = shift(back[:cut], 1), shift(ahead[cut:], -1)
    return jnp.stack([x, back]), jnp.stack([ahead, jnp.concatenate([head, tail], axis=0)])


def far_ring(low, high, shift):
    return [shift(low, 1), shift(high, 1), shift(low, -1), shift(high, -1)]


def close_far(low, high, came, shift):
    return [low, high, *came, shift(came[0], 1), shift(came[3], -1)]


def place(delta):
    return jnp.where(delta == 0, 0, jnp.where(delta == 3, 1, jnp.where(delta == 1, 2, 3)))


def local(near_blocks, leaf_basis, near_cols, near_count, children, parent_basis, far_coupling):
    leaves, slots = near_cols.shape
    row_index = lax.axis_index("row")
    col_index = lax.axis_index("col")
    row_count = lax.axis_size("row")
    col_count = lax.axis_size("col")
    side = 4
    group_size = leaves * col_count
    group_base = row_index * group_size

    def spot(offset):
        device = offset // 2
        z = place((device // side - col_index // side) % side)
        x = place((device % side - col_index % side) % side)
        return jnp.where(offset % 2 == 0, z * side + x, x * side + z)

    partner_row = row_index + 1 - 2 * (row_index % 2)
    parent_id = row_index * col_count + col_index
    partner_parent = partner_row * col_count + col_index
    child = jnp.stack([children[parent_id, 0], children[partner_parent, 1]]) - group_base
    where = jnp.stack([child % 2, spot(child)], axis=1).reshape(-1)
    offsets = (near_cols - group_base).reshape(-1)
    spots = spot(offsets)

    hold = lax.optimization_barrier
    first_way, second_way = ways(side)
    orders = ((first_way, second_way), (second_way, first_way))
    factors, pay, schur = diag_part(near_blocks, leaf_basis)
    near = [near_ring(pay[k], orders[k][0]) for k in range(2)]
    rows = [close_ring(pay[k], *near[k], orders[k][0]) for k in range(2)]
    own_pay, rows = hold((pay, rows))
    far = [far_ring(*rows[k], orders[k][1]) for k in range(2)]
    g = own_part(near_count, near_blocks, own_pay)
    g, far = hold((g, far))
    pieces = sum((close_far(*rows[k], far[k], orders[k][1]) for k in range(2)), [])
    first, outgoing = pick_part(where, pieces)
    second = lax.ppermute(outgoing, "row", [(r, r ^ 1) for r in range(row_count)])
    near_schur = near_part(offsets, spots, near_count, schur, g, pieces)
    top_factor, top_schur = top_part(first, second, far_coupling, parent_basis)
    return factors, near_schur, top_factor, top_schur


def solution(mesh):
    both = ("row", "col")
    return jax.shard_map(
        local,
        mesh=mesh,
        in_specs=(P(both), P(both), P(both), P(both), P(), P(both), P(both)),
        out_specs=(P(both), P(both), P(both), P(both)),
        check_vma=False,
    )
```

```python
from functools import partial

import jax
import jax.numpy as jnp
from jax import lax
from jax.experimental import pallas as pl
from jax.experimental.pallas import tpu as pltpu
from jax.sharding import PartitionSpec as P

F32 = jnp.float32
BF16 = jnp.bfloat16
LANE = 128
SUB = 8
HBM = pl.BlockSpec(memory_space=pltpu.HBM)
VMEM = pl.BlockSpec(memory_space=pltpu.VMEM)
SMEM = pl.BlockSpec(memory_space=pltpu.SMEM)
LARGE = pltpu.CompilerParams(vmem_limit_bytes=60 << 20)
STEP = 4


def guess(us):
    return pl.CostEstimate(flops=int(us * 1e9), bytes_accessed=0, transcendentals=0)


def split2(x):
    hi = x.astype(BF16)
    lo = (x - hi.astype(F32)).astype(BF16)
    return hi, lo


def dot(a, b):
    return jnp.dot(a, b, preferred_element_type=F32)


def dot_first(a, b):
    return lax.dot_general(a, b, (((0,), (0,)), ((), ())), preferred_element_type=F32)


def mul3(a, b, op=dot):
    ah, al = split2(a)
    bh, bl = split2(b)
    return op(ah, bh) + (op(ah, bl) + op(al, bh))


def spread(row):
    return jnp.broadcast_to(row, (SUB, row.shape[1]))


def lower_inverse(work, inv):
    n = LANE
    groups = 2
    width = groups * SUB
    row = lax.broadcasted_iota(jnp.int32, (n, n), 0)
    col = lax.broadcasted_iota(jnp.int32, (n, n), 1)
    eye = jnp.where(row == col, 1.0, 0.0).astype(F32)
    sub = lax.broadcasted_iota(jnp.int32, (SUB, n), 0)
    for t in inv:
        t[...] = eye
    for k in range(0, n, width):
        panels = []
        for a, t in zip(work, inv):
            pa = [a[k + g * SUB : k + (g + 1) * SUB, :] for g in range(groups)]
            pt = [t[k + g * SUB : k + (g + 1) * SUB, :] for g in range(groups)]
            cols = [
                [jnp.broadcast_to(pa[g][:, k + j : k + j + 1], (SUB, n)) for j in range((g + 1) * SUB)]
                for g in range(groups)
            ]
            panels.append((pa, pt, cols))
        for j in range(width):
            own, jj = divmod(j, SUB)
            for pa, pt, cols in panels:
                r = lax.rsqrt(spread(cols[own][j][jj : jj + 1]))
                r2 = r * r
                ra = spread(pa[own][jj : jj + 1]) * r
                rt = spread(pt[own][jj : jj + 1]) * r
                elems = {}
                for g in range(own, groups):
                    for m in range(max(j + 1, g * SUB), (g + 1) * SUB):
                        elems[m] = spread(cols[g][j][m - g * SUB : m - g * SUB + 1])
                for g in range(own, groups):
                    base = cols[g][j]
                    for m in range(j + 1, (g + 1) * SUB):
                        cols[g][m] = cols[g][m] - (base * elems[m]) * r2
                    c = base * r
                    if g == own:
                        c = jnp.where(sub > jj, c, 0.0)
                        pa[g] = jnp.where(sub == jj, ra, pa[g] - c * ra)
                        pt[g] = jnp.where(sub == jj, rt, pt[g] - c * rt)
                    else:
                        pa[g] = pa[g] - c * ra
                        pt[g] = pt[g] - c * rt
        for (pa, pt, _), a, t in zip(panels, work, inv):
            a_rows = jnp.concatenate(pa, axis=0)
            t_rows = jnp.concatenate(pt, axis=0)
            a[k : k + width, :] = a_rows
            t[k : k + width, :] = t_rows
            if k + width < n:
                hi, lo = split2(jnp.concatenate([a_rows, t_rows], axis=1))
                left = jnp.concatenate([hi[:, :n], hi[:, :n], lo[:, :n], lo[:, :n]], axis=0)
                right = jnp.concatenate([hi, lo, hi, lo], axis=0)
                upd = dot_first(left, right)
                a[k + width :, :] = a[k + width :, :] - upd[k + width :, :n]
                t[k + width :, :] = t[k + width :, :] - upd[k + width :, n:]


def pack_symmetric(m):
    n = LANE
    row = lax.broadcasted_iota(jnp.int32, (n, n), 0)
    col = lax.broadcasted_iota(jnp.int32, (n, n), 1)
    m = jnp.where(row >= col, m, m.T)
    hi = m.astype(BF16).astype(F32)
    lo = m - hi
    last = jnp.sum(jnp.where(row == col, lo, 0.0), axis=0, keepdims=True)
    body = jnp.where(row >= col, hi, lo)
    return jnp.concatenate([body, jnp.broadcast_to(last, (16, n))], axis=0).astype(BF16)


def unpack_symmetric(packed):
    n = LANE
    row = lax.broadcasted_iota(jnp.int32, (n, n), 0)
    col = lax.broadcasted_iota(jnp.int32, (n, n), 1)
    packed = packed.astype(F32)
    body = packed[:n]
    other = body.T
    last = jnp.broadcast_to(packed[n : n + 1], (n, n))
    return jnp.where(row == col, body + last, body + other)


def diag_kernel(a_ref, u_ref, factor_ref, schur_ref, *refs):
    pays, (w_ref, t_ref) = refs[:-2], refs[-2:]
    leaves = u_ref.shape[0]
    size = u_ref.shape[1]
    n = LANE
    blocks = size // n - 1
    red = blocks * n
    row = lax.broadcasted_iota(jnp.int32, (n, n), 0)
    col = lax.broadcasted_iota(jnp.int32, (n, n), 1)
    upper = row <= col
    for i in range(leaves):
        u = u_ref[i]
        hh, hl = split2(dot(a_ref[i, 0], u))
        w_ref[i] = dot_first(u, hh) + dot_first(u, hl)
    for b in range(blocks):
        lo, hi = b * n, (b + 1) * n
        lower_inverse(
            [w_ref.at[i, lo:hi, lo:hi] for i in range(leaves)],
            [t_ref.at[i, b] for i in range(leaves)],
        )
        for i in range(leaves):
            x = mul3(t_ref[i, b], w_ref[i, lo:hi, hi:])
            w_ref[i, lo:hi, hi:] = x
            xh, xl = split2(x)
            w_ref[i, hi:, hi:] = w_ref[i, hi:, hi:] - (
                dot_first(xh, xh) + (dot_first(xh, xl) + dot_first(xl, xh))
            )
    for i in range(leaves):
        schur = w_ref[i, red:, red:]
        schur_ref[i] = schur
        pays[i][:size, :] = u_ref[i, :, red:]
        pays[i][2 * size :, :] = pack_symmetric(schur)
        piv = [None] * blocks
        for b in reversed(range(blocks)):
            lo, hi = b * n, (b + 1) * n
            y = w_ref[i, lo:hi, red:]
            if b + 1 < blocks:
                y = y - mul3(w_ref[i, lo:hi, hi:red], jnp.concatenate(piv[b + 1 :], axis=0))
            piv[b] = mul3(t_ref[i, b], y, dot_first)
        ph, plo = split2(jnp.concatenate(piv, axis=0))
        ur = u_ref[i, :, :red]
        pays[i][size : 2 * size, :] = (dot(ur, ph) + dot(ur, plo)).astype(BF16)
        for b in range(blocks):
            for c in range(blocks):
                if c < b:
                    blk = w_ref[i, c * n : (c + 1) * n, b * n : (b + 1) * n].T
                elif c == b:
                    blk = jnp.where(upper, w_ref[i, b * n : (b + 1) * n, b * n : (b + 1) * n], 0.0).T
                else:
                    blk = jnp.zeros((n, n), F32)
                factor_ref[i, b * n : (b + 1) * n, c * n : (c + 1) * n] = blk


def diag_part(near_blocks, leaf_basis):
    leaves, size, _ = leaf_basis.shape
    red = size - LANE
    rows = 2 * size + LANE + 16
    return pl.pallas_call(
        diag_kernel,
        grid=(1,),
        in_specs=[
            pl.BlockSpec((leaves, 1, size, size), lambda g: (0, 0, 0, 0)),
            pl.BlockSpec((leaves, size, size), lambda g: (0, 0, 0)),
        ],
        out_specs=[
            pl.BlockSpec((leaves, red, red), lambda g: (0, 0, 0)),
            pl.BlockSpec((leaves, LANE, LANE), lambda g: (0, 0, 0)),
        ]
        + [pl.BlockSpec((rows, LANE), lambda g: (0, 0))] * leaves,
        out_shape=[
            jax.ShapeDtypeStruct((leaves, red, red), F32),
            jax.ShapeDtypeStruct((leaves, LANE, LANE), F32),
        ]
        + [jax.ShapeDtypeStruct((rows, LANE), BF16)] * leaves,
        scratch_shapes=[
            pltpu.VMEM((leaves, size, size), F32),
            pltpu.VMEM((leaves, size // LANE - 1, LANE, LANE), F32),
        ],
        compiler_params=LARGE,
        cost_estimate=guess(26),
        name="diag",
    )(near_blocks, leaf_basis)


def pick_kernel(where_ref, *refs):
    pieces, (first_ref, second_ref, sem) = refs[:-3], refs[-3:]
    rows = first_ref.shape[0]
    half = len(pieces) // 2
    for out, dst in enumerate((first_ref, second_ref)):
        base = 0
        for p, piece in enumerate(pieces):
            if p == half:
                base = 0
            count = piece.shape[0]
            leaf = 0 if p < half else 1
            slot = where_ref[2 * out + 1] - base

            @pl.when((where_ref[2 * out] == leaf) & (slot >= 0) & (slot < count))
            def _(piece=piece, slot=slot, dst=dst, out=out):
                at = jnp.clip(slot, 0, piece.shape[0] - 1)
                pltpu.make_async_copy(piece.at[at, pl.ds(piece.shape[1] - rows, rows)], dst, sem.at[out]).start()

            base += count
    for out, dst in enumerate((first_ref, second_ref)):
        pltpu.make_async_copy(pieces[0].at[0, pl.ds(pieces[0].shape[1] - rows, rows)], dst, sem.at[out]).wait()


def pick_part(where, pieces):
    rows = LANE + 16
    shape = jax.ShapeDtypeStruct((rows, LANE), BF16)
    return pl.pallas_call(
        pick_kernel,
        in_specs=[SMEM] + [HBM] * len(pieces),
        out_shape=[shape, shape],
        scratch_shapes=[pltpu.SemaphoreType.DMA((2,))],
        name="pick",
    )(where, *pieces)


def own_kernel(cnt_ref, a_hbm, *refs):
    pays, (g_hbm, a_buf, g_buf, left_ref, a_sem, g_sem) = refs[:-6], refs[-6:]
    leaves, slots, size, _ = a_hbm.shape

    def load(i, t):
        return pltpu.make_async_copy(a_hbm.at[i, t], a_buf.at[i, t], a_sem.at[i, t])

    def save(i, t):
        return pltpu.make_async_copy(g_buf.at[i, t], g_hbm.at[i, t], g_sem.at[i, t])

    for i in range(leaves):
        lax.fori_loop(1, cnt_ref[i], lambda t, _, i=i: load(i, t).start(), None)
    for i in range(leaves):
        left_ref[i, :LANE, :] = pays[i][:size].T
        left_ref[i, LANE:, :] = pays[i][size : 2 * size].T
    for i in range(leaves):

        def some(c, _, i=i):
            for t in [c * STEP + u for u in range(STEP)]:

                @pl.when((t > 0) & (t < cnt_ref[i]))
                def _(t=t):
                    load(i, t).wait()

            for t in [c * STEP + u for u in range(STEP)]:
                g = dot(left_ref[i], a_buf[i, t])
                g_s = g[:LANE]
                hi, lo = split2(g_s - g[LANE:])
                g_buf[i, t, 0] = hi
                g_buf[i, t, 1] = lo
                g_buf[i, t, 2] = g_s.astype(BF16)
            for t in [c * STEP + u for u in range(STEP)]:

                @pl.when((t > 0) & (t < cnt_ref[i]))
                def _(t=t):
                    save(i, t).start()

        lax.fori_loop(0, (cnt_ref[i] + (STEP - 1)) // STEP, some, None)
    for i in range(leaves):
        lax.fori_loop(1, cnt_ref[i], lambda t, _, i=i: save(i, t).wait(), None)


def own_part(counts, near_blocks, pays):
    leaves, slots, size, _ = near_blocks.shape
    shape = (leaves, slots, 3, LANE, size)
    return pl.pallas_call(
        own_kernel,
        in_specs=[SMEM, HBM] + [VMEM] * len(pays),
        out_specs=HBM,
        out_shape=jax.ShapeDtypeStruct(shape, BF16),
        scratch_shapes=[
            pltpu.VMEM(near_blocks.shape, BF16),
            pltpu.VMEM(shape, BF16),
            pltpu.VMEM((leaves, 2 * LANE, size), BF16),
            pltpu.SemaphoreType.DMA((leaves, slots)),
            pltpu.SemaphoreType.DMA((leaves, slots)),
        ],
        compiler_params=LARGE,
        cost_estimate=guess(8),
        name="own",
    )(counts, near_blocks, *pays)


def near_kernel(off_ref, spot_ref, cnt_ref, schur_ref, g_hbm, *refs):
    pieces, (out_ref, g_buf, r_buf, g_sem, r_sem) = refs[:-5], refs[-5:]
    leaves, slots = out_ref.shape[:2]
    rows = r_buf.shape[2]
    half = len(pieces) // 2
    count = pieces[0].shape[0]

    def load(i, t):
        return pltpu.make_async_copy(g_hbm.at[i, t], g_buf.at[i, t], g_sem.at[i, t])

    def fetch(i, t, piece, at):
        return pltpu.make_async_copy(piece.at[at, pl.ds(0, rows)], r_buf.at[i, t], r_sem.at[i, t])

    for i in range(leaves):

        def begin(t, _, i=i):
            load(i, t).start()
            at = i * slots + t
            spot = spot_ref[at]
            number = lax.rem(off_ref[at], 2) * half + lax.div(spot, count)
            for p, piece in enumerate(pieces):

                @pl.when(number == p)
                def _(piece=piece):
                    fetch(i, t, piece, lax.rem(spot, count)).start()

        lax.fori_loop(1, cnt_ref[i], begin, None)
    size = rows // 2
    for i in range(leaves):

        def some(c, _, i=i):
            for t in [c * STEP + u for u in range(STEP)]:

                @pl.when((t > 0) & (t < cnt_ref[i]))
                def _(t=t):
                    load(i, t).wait()
                    fetch(i, t, pieces[0], 0).wait()

            for t in [c * STEP + u for u in range(STEP)]:
                s_j = r_buf[i, t, :size]
                both = dot(g_buf[i, t, :2].reshape(2 * LANE, size), s_j)
                value = both[:LANE] + both[LANE:] - dot(g_buf[i, t, 2], r_buf[i, t, size:])
                out_ref[i, t] = jnp.where(t < cnt_ref[i], value, 0.0)

        def dead(t, _, i=i):
            out_ref[i, t] = jnp.zeros(out_ref.shape[2:], F32)

        steps = (cnt_ref[i] + (STEP - 1)) // STEP
        lax.fori_loop(0, steps, some, None)
        lax.fori_loop(steps * STEP, slots, dead, None)
        out_ref[i, 0] = schur_ref[i]


def near_part(offsets, spots, counts, schur, g, pieces):
    leaves, slots, _, _, size = g.shape
    return pl.pallas_call(
        near_kernel,
        in_specs=[SMEM, SMEM, SMEM, VMEM, HBM] + [HBM] * len(pieces),
        out_specs=VMEM,
        out_shape=jax.ShapeDtypeStruct((leaves, slots, LANE, LANE), F32),
        scratch_shapes=[
            pltpu.VMEM(g.shape, BF16),
            pltpu.VMEM((leaves, slots, 2 * size, LANE), BF16),
            pltpu.SemaphoreType.DMA((leaves, slots)),
            pltpu.SemaphoreType.DMA((leaves, slots)),
        ],
        compiler_params=LARGE,
        cost_estimate=guess(6),
        name="near",
    )(offsets, spots, counts, schur, g, *pieces)


def top_kernel(first_ref, second_ref, far_ref, v_ref, factor_ref, top_ref, w_ref, t_ref):
    n = LANE
    row = lax.broadcasted_iota(jnp.int32, (n, n), 0)
    col = lax.broadcasted_iota(jnp.int32, (n, n), 1)
    far = far_ref[0]
    merged = jnp.concatenate(
        [
            jnp.concatenate([unpack_symmetric(first_ref[...]), far], axis=1),
            jnp.concatenate([far.T, unpack_symmetric(second_ref[...])], axis=1),
        ],
        axis=0,
    )
    v = v_ref[0]
    mh, ml = split2(merged)
    hh, hl = split2(dot(mh, v) + dot(ml, v))
    p = dot_first(v, hh) + dot_first(v, hl)
    w_ref[...] = p[:n, :n]
    lower_inverse([w_ref], [t_ref])
    x = mul3(t_ref[...], p[:n, n:])
    top_ref[0] = p[n:, n:] - mul3(x, x, dot_first)
    factor_ref[0] = jnp.where(row <= col, w_ref[...], 0.0).T


def top_part(first, second, far, basis):
    shape = jax.ShapeDtypeStruct((1, LANE, LANE), F32)
    return pl.pallas_call(
        top_kernel,
        out_shape=[shape, shape],
        scratch_shapes=[pltpu.VMEM((LANE, LANE), F32), pltpu.VMEM((LANE, LANE), F32)],
        compiler_params=LARGE,
        cost_estimate=guess(8),
        name="top",
    )(first, second, far, basis)


def shifted(x, side, step_z, step_x):
    route = []
    for i in range(side * side):
        z, w = divmod(i, side)
        route.append((i, (z + step_z) % side * side + (w + step_x) % side))
    return lax.ppermute(x, "col", route)


def ways(side):
    def along_x(v, d):
        return shifted(v, side, 0, d)

    def along_z(v, d):
        return shifted(v, side, d, 0)

    return along_x, along_z


def near_ring(x, shift):
    return shift(x, 1), shift(x, -1)


def opposite(back, ahead, shift):
    cut = (back.shape[0] // 32 + 1) // 2 * 32
    return shift(back[:cut], 1), shift(ahead[cut:], -1)


def place(delta):
    return jnp.where(delta == 0, 0, jnp.where(delta == 3, 1, jnp.where(delta == 1, 2, 3)))


def local(near_blocks, leaf_basis, near_cols, near_count, children, parent_basis, far_coupling):
    leaves, slots = near_cols.shape
    row_index = lax.axis_index("row")
    col_index = lax.axis_index("col")
    row_count = lax.axis_size("row")
    col_count = lax.axis_size("col")
    side = 4
    group_size = leaves * col_count
    group_base = row_index * group_size

    def spot(offset):
        device = offset // 2
        z = place((device // side - col_index // side) % side)
        x = place((device % side - col_index % side) % side)
        return jnp.where(offset % 2 == 0, z * side + x, x * side + z)

    partner_row = row_index + 1 - 2 * (row_index % 2)
    parent_id = row_index * col_count + col_index
    partner_parent = partner_row * col_count + col_index
    child = jnp.stack([children[parent_id, 0], children[partner_parent, 1]]) - group_base
    where = jnp.stack([child % 2, spot(child)], axis=1).reshape(-1)
    offsets = (near_cols - group_base).reshape(-1)
    spots = spot(offsets)

    hold = lax.optimization_barrier
    first_way, second_way = ways(side)
    orders = ((first_way, second_way), (second_way, first_way))
    factors, schur, *pays = diag_part(near_blocks, leaf_basis)
    near = [near_ring(pays[k], orders[k][0]) for k in range(2)]
    parts = [opposite(*near[k], orders[k][0]) for k in range(2)]
    low = [jnp.stack([pays[k], near[k][0]]) for k in range(2)]
    low_far = [near_ring(low[k], orders[k][1]) for k in range(2)]
    own_pays, _ = hold((pays, low))
    g = own_part(near_count, near_blocks, own_pays)
    ahead = [near[k][1] for k in range(2)]
    g, ahead, parts = hold((g, ahead, parts))
    high = [jnp.stack([ahead[k], jnp.concatenate(parts[k], axis=0)]) for k in range(2)]
    high_far = [near_ring(high[k], orders[k][1]) for k in range(2)]
    pieces = []
    for k in range(2):
        shift = orders[k][1]
        pieces += [low[k], high[k], low_far[k][0], high_far[k][0], low_far[k][1], high_far[k][1]]
        pieces += [shift(low_far[k][0], 1), shift(high_far[k][1], -1)]
    first, outgoing = pick_part(where, pieces)
    second = lax.ppermute(outgoing, "row", [(r, r ^ 1) for r in range(row_count)])
    near_schur = near_part(offsets, spots, near_count, schur, g, pieces)
    top_factor, top_schur = top_part(first, second, far_coupling, parent_basis)
    return factors, near_schur, top_factor, top_schur


def solution(mesh):
    both = ("row", "col")
    return jax.shard_map(
        local,
        mesh=mesh,
        in_specs=(P(both), P(both), P(both), P(both), P(), P(both), P(both)),
        out_specs=(P(both), P(both), P(both), P(both)),
        check_vma=False,
    )
```

```python
from functools import partial

import jax
import jax.numpy as jnp
from jax import lax
from jax.experimental import pallas as pl
from jax.experimental.pallas import tpu as pltpu
from jax.sharding import PartitionSpec as P

F32 = jnp.float32
BF16 = jnp.bfloat16
LANE = 128
SUB = 8
HBM = pl.BlockSpec(memory_space=pltpu.HBM)
VMEM = pl.BlockSpec(memory_space=pltpu.VMEM)
SMEM = pl.BlockSpec(memory_space=pltpu.SMEM)
LARGE = pltpu.CompilerParams(vmem_limit_bytes=60 << 20)
STEP = 4


def guess(us):
    return pl.CostEstimate(flops=int(us * 1e9), bytes_accessed=0, transcendentals=0)


def split2(x):
    hi = x.astype(BF16)
    lo = (x - hi.astype(F32)).astype(BF16)
    return hi, lo


def dot(a, b):
    return jnp.dot(a, b, preferred_element_type=F32)


def dot_first(a, b):
    return lax.dot_general(a, b, (((0,), (0,)), ((), ())), preferred_element_type=F32)


def mul3(a, b, op=dot):
    ah, al = split2(a)
    bh, bl = split2(b)
    return op(ah, bh) + (op(ah, bl) + op(al, bh))


def spread(row):
    return jnp.broadcast_to(row, (SUB, row.shape[1]))


def lower_inverse(work, inv):
    n = LANE
    groups = 2
    width = groups * SUB
    row = lax.broadcasted_iota(jnp.int32, (n, n), 0)
    col = lax.broadcasted_iota(jnp.int32, (n, n), 1)
    eye = jnp.where(row == col, 1.0, 0.0).astype(F32)
    sub = lax.broadcasted_iota(jnp.int32, (SUB, n), 0)
    for t in inv:
        t[...] = eye
    for k in range(0, n, width):
        panels = []
        for a, t in zip(work, inv):
            pa = [a[k + g * SUB : k + (g + 1) * SUB, :] for g in range(groups)]
            pt = [t[k + g * SUB : k + (g + 1) * SUB, :] for g in range(groups)]
            cols = [
                [jnp.broadcast_to(pa[g][:, k + j : k + j + 1], (SUB, n)) for j in range((g + 1) * SUB)]
                for g in range(groups)
            ]
            panels.append((pa, pt, cols))
        for j in range(width):
            own, jj = divmod(j, SUB)
            for pa, pt, cols in panels:
                r = lax.rsqrt(spread(cols[own][j][jj : jj + 1]))
                r2 = r * r
                ra = spread(pa[own][jj : jj + 1]) * r
                rt = spread(pt[own][jj : jj + 1]) * r
                elems = {}
                for g in range(own, groups):
                    for m in range(max(j + 1, g * SUB), (g + 1) * SUB):
                        elems[m] = spread(cols[g][j][m - g * SUB : m - g * SUB + 1])
                for g in range(own, groups):
                    base = cols[g][j]
                    for m in range(j + 1, (g + 1) * SUB):
                        cols[g][m] = cols[g][m] - (base * elems[m]) * r2
                    c = base * r
                    if g == own:
                        c = jnp.where(sub > jj, c, 0.0)
                        pa[g] = jnp.where(sub == jj, ra, pa[g] - c * ra)
                        pt[g] = jnp.where(sub == jj, rt, pt[g] - c * rt)
                    else:
                        pa[g] = pa[g] - c * ra
                        pt[g] = pt[g] - c * rt
        for (pa, pt, _), a, t in zip(panels, work, inv):
            a_rows = jnp.concatenate(pa, axis=0)
            t_rows = jnp.concatenate(pt, axis=0)
            a[k : k + width, :] = a_rows
            t[k : k + width, :] = t_rows
            if k + width < n:
                hi, lo = split2(jnp.concatenate([a_rows, t_rows], axis=1))
                left = jnp.concatenate([hi[:, :n], hi[:, :n], lo[:, :n], lo[:, :n]], axis=0)
                right = jnp.concatenate([hi, lo, hi, lo], axis=0)
                upd = dot_first(left, right)
                a[k + width :, :] = a[k + width :, :] - upd[k + width :, :n]
                t[k + width :, :] = t[k + width :, :] - upd[k + width :, n:]


def pack_symmetric(m):
    n = LANE
    row = lax.broadcasted_iota(jnp.int32, (n, n), 0)
    col = lax.broadcasted_iota(jnp.int32, (n, n), 1)
    m = jnp.where(row >= col, m, m.T)
    hi = m.astype(BF16).astype(F32)
    lo = m - hi
    last = jnp.sum(jnp.where(row == col, lo, 0.0), axis=0, keepdims=True)
    body = jnp.where(row >= col, hi, lo)
    return jnp.concatenate([body, jnp.broadcast_to(last, (16, n))], axis=0).astype(BF16)


def unpack_symmetric(packed):
    n = LANE
    row = lax.broadcasted_iota(jnp.int32, (n, n), 0)
    col = lax.broadcasted_iota(jnp.int32, (n, n), 1)
    packed = packed.astype(F32)
    body = packed[:n]
    other = body.T
    last = jnp.broadcast_to(packed[n : n + 1], (n, n))
    return jnp.where(row == col, body + last, body + other)


def diag_kernel(a_ref, u_ref, factor_ref, schur_ref, *refs):
    pays, (w_ref, t_ref) = refs[:-2], refs[-2:]
    leaves = u_ref.shape[0]
    size = u_ref.shape[1]
    n = LANE
    blocks = size // n - 1
    red = blocks * n
    row = lax.broadcasted_iota(jnp.int32, (n, n), 0)
    col = lax.broadcasted_iota(jnp.int32, (n, n), 1)
    upper = row <= col
    for i in range(leaves):
        u = u_ref[i]
        hh, hl = split2(dot(a_ref[i, 0], u))
        w_ref[i] = dot_first(u, hh) + dot_first(u, hl)
    for b in range(blocks):
        lo, hi = b * n, (b + 1) * n
        lower_inverse(
            [w_ref.at[i, lo:hi, lo:hi] for i in range(leaves)],
            [t_ref.at[i, b] for i in range(leaves)],
        )
        for i in range(leaves):
            x = mul3(t_ref[i, b], w_ref[i, lo:hi, hi:])
            w_ref[i, lo:hi, hi:] = x
            xh, xl = split2(x)
            w_ref[i, hi:, hi:] = w_ref[i, hi:, hi:] - (
                dot_first(xh, xh) + (dot_first(xh, xl) + dot_first(xl, xh))
            )
    for i in range(leaves):
        schur = w_ref[i, red:, red:]
        schur_ref[i] = schur
        pays[i][:size, :] = u_ref[i, :, red:]
        pays[i][2 * size :, :] = pack_symmetric(schur)
        piv = [None] * blocks
        for b in reversed(range(blocks)):
            lo, hi = b * n, (b + 1) * n
            y = w_ref[i, lo:hi, red:]
            if b + 1 < blocks:
                y = y - mul3(w_ref[i, lo:hi, hi:red], jnp.concatenate(piv[b + 1 :], axis=0))
            piv[b] = mul3(t_ref[i, b], y, dot_first)
        ph, plo = split2(jnp.concatenate(piv, axis=0))
        ur = u_ref[i, :, :red]
        pays[i][size : 2 * size, :] = (dot(ur, ph) + dot(ur, plo)).astype(BF16)
        for b in range(blocks):
            for c in range(blocks):
                if c < b:
                    blk = w_ref[i, c * n : (c + 1) * n, b * n : (b + 1) * n].T
                elif c == b:
                    blk = jnp.where(upper, w_ref[i, b * n : (b + 1) * n, b * n : (b + 1) * n], 0.0).T
                else:
                    blk = jnp.zeros((n, n), F32)
                factor_ref[i, b * n : (b + 1) * n, c * n : (c + 1) * n] = blk


def diag_part(near_blocks, leaf_basis):
    leaves, size, _ = leaf_basis.shape
    red = size - LANE
    rows = 2 * size + LANE + 16
    return pl.pallas_call(
        diag_kernel,
        grid=(1,),
        in_specs=[
            pl.BlockSpec((leaves, 1, size, size), lambda g: (0, 0, 0, 0)),
            pl.BlockSpec((leaves, size, size), lambda g: (0, 0, 0)),
        ],
        out_specs=[
            pl.BlockSpec((leaves, red, red), lambda g: (0, 0, 0)),
            pl.BlockSpec((leaves, LANE, LANE), lambda g: (0, 0, 0)),
        ]
        + [pl.BlockSpec((rows, LANE), lambda g: (0, 0))] * leaves,
        out_shape=[
            jax.ShapeDtypeStruct((leaves, red, red), F32),
            jax.ShapeDtypeStruct((leaves, LANE, LANE), F32),
        ]
        + [jax.ShapeDtypeStruct((rows, LANE), BF16)] * leaves,
        scratch_shapes=[
            pltpu.VMEM((leaves, size, size), F32),
            pltpu.VMEM((leaves, size // LANE - 1, LANE, LANE), F32),
        ],
        compiler_params=LARGE,
        cost_estimate=guess(26),
        name="diag",
    )(near_blocks, leaf_basis)


def pick_kernel(where_ref, *refs):
    pieces, (first_ref, second_ref, sem) = refs[:-3], refs[-3:]
    rows = first_ref.shape[0]
    half = len(pieces) // 2
    for out, dst in enumerate((first_ref, second_ref)):
        base = 0
        for p, piece in enumerate(pieces):
            if p == half:
                base = 0
            count = piece.shape[0]
            leaf = 0 if p < half else 1
            slot = where_ref[2 * out + 1] - base

            @pl.when((where_ref[2 * out] == leaf) & (slot >= 0) & (slot < count))
            def _(piece=piece, slot=slot, dst=dst, out=out):
                at = jnp.clip(slot, 0, piece.shape[0] - 1)
                pltpu.make_async_copy(piece.at[at, pl.ds(piece.shape[1] - rows, rows)], dst, sem.at[out]).start()

            base += count
    for out, dst in enumerate((first_ref, second_ref)):
        pltpu.make_async_copy(pieces[0].at[0, pl.ds(pieces[0].shape[1] - rows, rows)], dst, sem.at[out]).wait()


def pick_part(where, pieces):
    rows = LANE + 16
    shape = jax.ShapeDtypeStruct((rows, LANE), BF16)
    return pl.pallas_call(
        pick_kernel,
        in_specs=[SMEM] + [HBM] * len(pieces),
        out_shape=[shape, shape],
        scratch_shapes=[pltpu.SemaphoreType.DMA((2,))],
        name="pick",
    )(where, *pieces)


def own_kernel(cnt_ref, a_hbm, *refs):
    pays, (g_hbm, a_buf, g_buf, left_ref, a_sem, g_sem) = refs[:-6], refs[-6:]
    leaves, slots, size, _ = a_hbm.shape

    def load(i, t):
        return pltpu.make_async_copy(a_hbm.at[i, t], a_buf.at[i, t], a_sem.at[i, t])

    def save(i, t):
        return pltpu.make_async_copy(g_buf.at[i, t], g_hbm.at[i, t], g_sem.at[i, t])

    for i in range(leaves):
        lax.fori_loop(1, cnt_ref[i], lambda t, _, i=i: load(i, t).start(), None)
    for i in range(leaves):
        left_ref[i, :LANE, :] = pays[i][:size].T
        left_ref[i, LANE:, :] = pays[i][size : 2 * size].T
    for i in range(leaves):

        def some(c, _, i=i):
            for t in [c * STEP + u for u in range(STEP)]:

                @pl.when((t > 0) & (t < cnt_ref[i]))
                def _(t=t):
                    load(i, t).wait()

            for t in [c * STEP + u for u in range(STEP)]:
                g = dot(left_ref[i], a_buf[i, t])
                g_s = g[:LANE]
                hi, lo = split2(g_s - g[LANE:])
                g_buf[i, t, 0] = hi
                g_buf[i, t, 1] = lo
                g_buf[i, t, 2] = g_s.astype(BF16)
            for t in [c * STEP + u for u in range(STEP)]:

                @pl.when((t > 0) & (t < cnt_ref[i]))
                def _(t=t):
                    save(i, t).start()

        lax.fori_loop(0, (cnt_ref[i] + (STEP - 1)) // STEP, some, None)
    for i in range(leaves):
        lax.fori_loop(1, cnt_ref[i], lambda t, _, i=i: save(i, t).wait(), None)


def own_part(counts, near_blocks, pays):
    leaves, slots, size, _ = near_blocks.shape
    shape = (leaves, slots, 3, LANE, size)
    return pl.pallas_call(
        own_kernel,
        in_specs=[SMEM, HBM] + [VMEM] * len(pays),
        out_specs=HBM,
        out_shape=jax.ShapeDtypeStruct(shape, BF16),
        scratch_shapes=[
            pltpu.VMEM(near_blocks.shape, BF16),
            pltpu.VMEM(shape, BF16),
            pltpu.VMEM((leaves, 2 * LANE, size), BF16),
            pltpu.SemaphoreType.DMA((leaves, slots)),
            pltpu.SemaphoreType.DMA((leaves, slots)),
        ],
        compiler_params=LARGE,
        cost_estimate=guess(8),
        name="own",
    )(counts, near_blocks, *pays)


def near_kernel(off_ref, spot_ref, cnt_ref, schur_ref, g_hbm, *refs):
    pieces, (out_ref, g_buf, r_buf, g_sem, r_sem) = refs[:-5], refs[-5:]
    leaves, slots = out_ref.shape[:2]
    rows = r_buf.shape[2]
    half = len(pieces) // 2
    count = pieces[0].shape[0]

    def load(i, t):
        return pltpu.make_async_copy(g_hbm.at[i, t], g_buf.at[i, t], g_sem.at[i, t])

    def fetch(i, t, piece, at):
        return pltpu.make_async_copy(piece.at[at, pl.ds(0, rows)], r_buf.at[i, t], r_sem.at[i, t])

    for i in range(leaves):

        def begin(t, _, i=i):
            load(i, t).start()
            at = i * slots + t
            spot = spot_ref[at]
            number = lax.rem(off_ref[at], 2) * half + lax.div(spot, count)
            for p, piece in enumerate(pieces):

                @pl.when(number == p)
                def _(piece=piece):
                    fetch(i, t, piece, lax.rem(spot, count)).start()

        lax.fori_loop(1, cnt_ref[i], begin, None)
    size = rows // 2
    for i in range(leaves):

        def some(c, _, i=i):
            for t in [c * STEP + u for u in range(STEP)]:

                @pl.when((t > 0) & (t < cnt_ref[i]))
                def _(t=t):
                    load(i, t).wait()
                    fetch(i, t, pieces[0], 0).wait()

            for t in [c * STEP + u for u in range(STEP)]:
                s_j = r_buf[i, t, :size]
                both = dot(g_buf[i, t, :2].reshape(2 * LANE, size), s_j)
                value = both[:LANE] + both[LANE:] - dot(g_buf[i, t, 2], r_buf[i, t, size:])
                out_ref[i, t] = jnp.where(t < cnt_ref[i], value, 0.0)

        def dead(t, _, i=i):
            out_ref[i, t] = jnp.zeros(out_ref.shape[2:], F32)

        steps = (cnt_ref[i] + (STEP - 1)) // STEP
        lax.fori_loop(0, steps, some, None)
        lax.fori_loop(steps * STEP, slots, dead, None)
        out_ref[i, 0] = schur_ref[i]


def near_part(offsets, spots, counts, schur, g, pieces):
    leaves, slots, _, _, size = g.shape
    return pl.pallas_call(
        near_kernel,
        in_specs=[SMEM, SMEM, SMEM, VMEM, HBM] + [HBM] * len(pieces),
        out_specs=VMEM,
        out_shape=jax.ShapeDtypeStruct((leaves, slots, LANE, LANE), F32),
        scratch_shapes=[
            pltpu.VMEM(g.shape, BF16),
            pltpu.VMEM((leaves, slots, 2 * size, LANE), BF16),
            pltpu.SemaphoreType.DMA((leaves, slots)),
            pltpu.SemaphoreType.DMA((leaves, slots)),
        ],
        compiler_params=LARGE,
        cost_estimate=guess(6),
        name="near",
    )(offsets, spots, counts, schur, g, *pieces)


def top_kernel(first_ref, second_ref, far_ref, v_ref, factor_ref, top_ref, w_ref, t_ref):
    n = LANE
    row = lax.broadcasted_iota(jnp.int32, (n, n), 0)
    col = lax.broadcasted_iota(jnp.int32, (n, n), 1)
    far = far_ref[0]
    merged = jnp.concatenate(
        [
            jnp.concatenate([unpack_symmetric(first_ref[...]), far], axis=1),
            jnp.concatenate([far.T, unpack_symmetric(second_ref[...])], axis=1),
        ],
        axis=0,
    )
    v = v_ref[0]
    mh, ml = split2(merged)
    hh, hl = split2(dot(mh, v) + dot(ml, v))
    p = dot_first(v, hh) + dot_first(v, hl)
    w_ref[...] = p[:n, :n]
    lower_inverse([w_ref], [t_ref])
    x = mul3(t_ref[...], p[:n, n:])
    top_ref[0] = p[n:, n:] - mul3(x, x, dot_first)
    factor_ref[0] = jnp.where(row <= col, w_ref[...], 0.0).T


def top_part(first, second, far, basis):
    shape = jax.ShapeDtypeStruct((1, LANE, LANE), F32)
    return pl.pallas_call(
        top_kernel,
        out_shape=[shape, shape],
        scratch_shapes=[pltpu.VMEM((LANE, LANE), F32), pltpu.VMEM((LANE, LANE), F32)],
        compiler_params=LARGE,
        cost_estimate=guess(8),
        name="top",
    )(first, second, far, basis)


def shifted(x, side, step_z, step_x):
    route = []
    for i in range(side * side):
        z, w = divmod(i, side)
        route.append((i, (z + step_z) % side * side + (w + step_x) % side))
    return lax.ppermute(x, "col", route)


def ways(side):
    def along_x(v, d):
        return shifted(v, side, 0, d)

    def along_z(v, d):
        return shifted(v, side, d, 0)

    return along_x, along_z


def near_ring(x, shift):
    return shift(x, 1), shift(x, -1)


def place(delta):
    return jnp.where(delta == 0, 0, jnp.where(delta == 3, 1, jnp.where(delta == 1, 2, 3)))


def local(near_blocks, leaf_basis, near_cols, near_count, children, parent_basis, far_coupling):
    leaves, slots = near_cols.shape
    row_index = lax.axis_index("row")
    col_index = lax.axis_index("col")
    row_count = lax.axis_size("row")
    col_count = lax.axis_size("col")
    side = 4
    group_size = leaves * col_count
    group_base = row_index * group_size

    def spot(offset):
        device = offset // 2
        z = place((device // side - col_index // side) % side)
        x = place((device % side - col_index % side) % side)
        return jnp.where(offset % 2 == 0, z * side + x, x * side + z)

    partner_row = row_index + 1 - 2 * (row_index % 2)
    parent_id = row_index * col_count + col_index
    partner_parent = partner_row * col_count + col_index
    child = jnp.stack([children[parent_id, 0], children[partner_parent, 1]]) - group_base
    where = jnp.stack([child % 2, spot(child)], axis=1).reshape(-1)
    offsets = (near_cols - group_base).reshape(-1)
    spots = spot(offsets)

    hold = lax.optimization_barrier
    first_way, second_way = ways(side)
    orders = ((first_way, second_way), (second_way, first_way))
    factors, schur, *pays = diag_part(near_blocks, leaf_basis)
    near = [near_ring(pays[k], orders[k][0]) for k in range(2)]
    low = [jnp.stack([pays[k], near[k][0]]) for k in range(2)]
    low_far = [near_ring(low[k], orders[k][1]) for k in range(2)]
    far = [orders[0][0](near[0][0], 1), orders[1][0](near[1][1], -1)]
    own_pays, _ = hold((pays, low))
    g = own_part(near_count, near_blocks, own_pays)
    g, ahead, far = hold((g, [near[k][1] for k in range(2)], far))
    high = [jnp.stack([ahead[k], far[k]]) for k in range(2)]
    high_far = [near_ring(high[k], orders[k][1]) for k in range(2)]
    pieces = []
    for k in range(2):
        shift = orders[k][1]
        pieces += [low[k], high[k], low_far[k][0], high_far[k][0], low_far[k][1], high_far[k][1]]
        pieces += [shift(low_far[k][0], 1), shift(high_far[k][1], -1)]
    first, outgoing = pick_part(where, pieces)
    second = lax.ppermute(outgoing, "row", [(r, r ^ 1) for r in range(row_count)])
    near_schur = near_part(offsets, spots, near_count, schur, g, pieces)
    top_factor, top_schur = top_part(first, second, far_coupling, parent_basis)
    return factors, near_schur, top_factor, top_schur


def solution(mesh):
    both = ("row", "col")
    return jax.shard_map(
        local,
        mesh=mesh,
        in_specs=(P(both), P(both), P(both), P(both), P(), P(both), P(both)),
        out_specs=(P(both), P(both), P(both), P(both)),
        check_vma=False,
    )
```

```python
from functools import partial

import jax
import jax.numpy as jnp
from jax import lax
from jax.experimental import pallas as pl
from jax.experimental.pallas import tpu as pltpu
from jax.sharding import PartitionSpec as P

F32 = jnp.float32
BF16 = jnp.bfloat16
LANE = 128
SUB = 8
HBM = pl.BlockSpec(memory_space=pltpu.HBM)
VMEM = pl.BlockSpec(memory_space=pltpu.VMEM)
SMEM = pl.BlockSpec(memory_space=pltpu.SMEM)
LARGE = pltpu.CompilerParams(vmem_limit_bytes=60 << 20)
STEP = 4


def guess(us):
    return pl.CostEstimate(flops=int(us * 1e9), bytes_accessed=0, transcendentals=0)


def split2(x):
    hi = x.astype(BF16)
    lo = (x - hi.astype(F32)).astype(BF16)
    return hi, lo


def dot(a, b):
    return jnp.dot(a, b, preferred_element_type=F32)


def dot_first(a, b):
    return lax.dot_general(a, b, (((0,), (0,)), ((), ())), preferred_element_type=F32)


def mul3(a, b, op=dot):
    ah, al = split2(a)
    bh, bl = split2(b)
    return op(ah, bh) + (op(ah, bl) + op(al, bh))


def spread(row):
    return jnp.broadcast_to(row, (SUB, row.shape[1]))


def lower_inverse(work, inv):
    n = LANE
    groups = 2
    width = groups * SUB
    row = lax.broadcasted_iota(jnp.int32, (n, n), 0)
    col = lax.broadcasted_iota(jnp.int32, (n, n), 1)
    eye = jnp.where(row == col, 1.0, 0.0).astype(F32)
    sub = lax.broadcasted_iota(jnp.int32, (SUB, n), 0)
    for t in inv:
        t[...] = eye
    for k in range(0, n, width):
        panels = []
        for a, t in zip(work, inv):
            pa = [a[k + g * SUB : k + (g + 1) * SUB, :] for g in range(groups)]
            pt = [t[k + g * SUB : k + (g + 1) * SUB, :] for g in range(groups)]
            cols = [
                [jnp.broadcast_to(pa[g][:, k + j : k + j + 1], (SUB, n)) for j in range((g + 1) * SUB)]
                for g in range(groups)
            ]
            panels.append((pa, pt, cols))
        for j in range(width):
            own, jj = divmod(j, SUB)
            for pa, pt, cols in panels:
                r = lax.rsqrt(spread(cols[own][j][jj : jj + 1]))
                r2 = r * r
                ra = spread(pa[own][jj : jj + 1]) * r
                rt = spread(pt[own][jj : jj + 1]) * r
                elems = {}
                for g in range(own, groups):
                    for m in range(max(j + 1, g * SUB), (g + 1) * SUB):
                        elems[m] = spread(cols[g][j][m - g * SUB : m - g * SUB + 1])
                for g in range(own, groups):
                    base = cols[g][j]
                    for m in range(j + 1, (g + 1) * SUB):
                        cols[g][m] = cols[g][m] - (base * elems[m]) * r2
                    c = base * r
                    if g == own:
                        c = jnp.where(sub > jj, c, 0.0)
                        pa[g] = jnp.where(sub == jj, ra, pa[g] - c * ra)
                        pt[g] = jnp.where(sub == jj, rt, pt[g] - c * rt)
                    else:
                        pa[g] = pa[g] - c * ra
                        pt[g] = pt[g] - c * rt
        for (pa, pt, _), a, t in zip(panels, work, inv):
            a_rows = jnp.concatenate(pa, axis=0)
            t_rows = jnp.concatenate(pt, axis=0)
            a[k : k + width, :] = a_rows
            t[k : k + width, :] = t_rows
            if k + width < n:
                hi, lo = split2(jnp.concatenate([a_rows, t_rows], axis=1))
                left = jnp.concatenate([hi[:, :n], hi[:, :n], lo[:, :n], lo[:, :n]], axis=0)
                right = jnp.concatenate([hi, lo, hi, lo], axis=0)
                upd = dot_first(left, right)
                a[k + width :, :] = a[k + width :, :] - upd[k + width :, :n]
                t[k + width :, :] = t[k + width :, :] - upd[k + width :, n:]


def pack_symmetric(m):
    n = LANE
    row = lax.broadcasted_iota(jnp.int32, (n, n), 0)
    col = lax.broadcasted_iota(jnp.int32, (n, n), 1)
    m = jnp.where(row >= col, m, m.T)
    hi = m.astype(BF16).astype(F32)
    lo = m - hi
    last = jnp.sum(jnp.where(row == col, lo, 0.0), axis=0, keepdims=True)
    body = jnp.where(row >= col, hi, lo)
    return jnp.concatenate([body, jnp.broadcast_to(last, (16, n))], axis=0).astype(BF16)


def unpack_symmetric(packed):
    n = LANE
    row = lax.broadcasted_iota(jnp.int32, (n, n), 0)
    col = lax.broadcasted_iota(jnp.int32, (n, n), 1)
    packed = packed.astype(F32)
    body = packed[:n]
    other = body.T
    last = jnp.broadcast_to(packed[n : n + 1], (n, n))
    return jnp.where(row == col, body + last, body + other)


def diag_kernel(a_ref, u_ref, factor_ref, schur_ref, *refs):
    pays, (w_ref, t_ref) = refs[:-2], refs[-2:]
    leaves = u_ref.shape[0]
    size = u_ref.shape[1]
    n = LANE
    blocks = size // n - 1
    red = blocks * n
    row = lax.broadcasted_iota(jnp.int32, (n, n), 0)
    col = lax.broadcasted_iota(jnp.int32, (n, n), 1)
    upper = row <= col
    for i in range(leaves):
        u = u_ref[i]
        hh, hl = split2(dot(a_ref[i, 0], u))
        w_ref[i] = dot_first(u, hh) + dot_first(u, hl)
    for b in range(blocks):
        lo, hi = b * n, (b + 1) * n
        lower_inverse(
            [w_ref.at[i, lo:hi, lo:hi] for i in range(leaves)],
            [t_ref.at[i, b] for i in range(leaves)],
        )
        for i in range(leaves):
            x = mul3(t_ref[i, b], w_ref[i, lo:hi, hi:])
            w_ref[i, lo:hi, hi:] = x
            xh, xl = split2(x)
            w_ref[i, hi:, hi:] = w_ref[i, hi:, hi:] - (
                dot_first(xh, xh) + (dot_first(xh, xl) + dot_first(xl, xh))
            )
    for i in range(leaves):
        schur = w_ref[i, red:, red:]
        schur_ref[i] = schur
        pays[i][:size, :] = u_ref[i, :, red:]
        pays[i][2 * size :, :] = pack_symmetric(schur)
        piv = [None] * blocks
        for b in reversed(range(blocks)):
            lo, hi = b * n, (b + 1) * n
            y = w_ref[i, lo:hi, red:]
            if b + 1 < blocks:
                y = y - mul3(w_ref[i, lo:hi, hi:red], jnp.concatenate(piv[b + 1 :], axis=0))
            piv[b] = mul3(t_ref[i, b], y, dot_first)
        ph, plo = split2(jnp.concatenate(piv, axis=0))
        ur = u_ref[i, :, :red]
        pays[i][size : 2 * size, :] = (dot(ur, ph) + dot(ur, plo)).astype(BF16)
        for b in range(blocks):
            for c in range(blocks):
                if c < b:
                    blk = w_ref[i, c * n : (c + 1) * n, b * n : (b + 1) * n].T
                elif c == b:
                    blk = jnp.where(upper, w_ref[i, b * n : (b + 1) * n, b * n : (b + 1) * n], 0.0).T
                else:
                    blk = jnp.zeros((n, n), F32)
                factor_ref[i, b * n : (b + 1) * n, c * n : (c + 1) * n] = blk


def diag_part(near_blocks, leaf_basis):
    leaves, size, _ = leaf_basis.shape
    red = size - LANE
    rows = 2 * size + LANE + 16
    return pl.pallas_call(
        diag_kernel,
        grid=(1,),
        in_specs=[
            pl.BlockSpec((leaves, 1, size, size), lambda g: (0, 0, 0, 0)),
            pl.BlockSpec((leaves, size, size), lambda g: (0, 0, 0)),
        ],
        out_specs=[
            pl.BlockSpec((leaves, red, red), lambda g: (0, 0, 0)),
            pl.BlockSpec((leaves, LANE, LANE), lambda g: (0, 0, 0)),
        ]
        + [pl.BlockSpec((rows, LANE), lambda g: (0, 0))] * leaves,
        out_shape=[
            jax.ShapeDtypeStruct((leaves, red, red), F32),
            jax.ShapeDtypeStruct((leaves, LANE, LANE), F32),
        ]
        + [jax.ShapeDtypeStruct((rows, LANE), BF16)] * leaves,
        scratch_shapes=[
            pltpu.VMEM((leaves, size, size), F32),
            pltpu.VMEM((leaves, size // LANE - 1, LANE, LANE), F32),
        ],
        compiler_params=LARGE,
        cost_estimate=guess(26),
        name="diag",
    )(near_blocks, leaf_basis)


def pick_kernel(where_ref, *refs):
    pieces, (first_ref, second_ref, sem) = refs[:-3], refs[-3:]
    rows = first_ref.shape[0]
    half = len(pieces) // 2
    for out, dst in enumerate((first_ref, second_ref)):
        base = 0
        for p, piece in enumerate(pieces):
            if p == half:
                base = 0
            count = piece.shape[0]
            leaf = 0 if p < half else 1
            slot = where_ref[2 * out + 1] - base

            @pl.when((where_ref[2 * out] == leaf) & (slot >= 0) & (slot < count))
            def _(piece=piece, slot=slot, dst=dst, out=out):
                at = jnp.clip(slot, 0, piece.shape[0] - 1)
                pltpu.make_async_copy(piece.at[at, pl.ds(piece.shape[1] - rows, rows)], dst, sem.at[out]).start()

            base += count
    for out, dst in enumerate((first_ref, second_ref)):
        pltpu.make_async_copy(pieces[0].at[0, pl.ds(pieces[0].shape[1] - rows, rows)], dst, sem.at[out]).wait()


def pick_part(where, pieces):
    rows = LANE + 16
    shape = jax.ShapeDtypeStruct((rows, LANE), BF16)
    return pl.pallas_call(
        pick_kernel,
        in_specs=[SMEM] + [HBM] * len(pieces),
        out_shape=[shape, shape],
        scratch_shapes=[pltpu.SemaphoreType.DMA((2,))],
        name="pick",
    )(where, *pieces)


def own_kernel(cnt_ref, a_hbm, *refs):
    pays, (g_hbm, a_buf, g_buf, left_ref, a_sem, g_sem) = refs[:-6], refs[-6:]
    leaves, slots, size, _ = a_hbm.shape

    def load(i, t):
        return pltpu.make_async_copy(a_hbm.at[i, t], a_buf.at[i, t], a_sem.at[i, t])

    def save(i, t):
        return pltpu.make_async_copy(g_buf.at[i, t], g_hbm.at[i, t], g_sem.at[i, t])

    for i in range(leaves):
        lax.fori_loop(1, cnt_ref[i], lambda t, _, i=i: load(i, t).start(), None)
    for i in range(leaves):
        left_ref[i, :LANE, :] = pays[i][:size].T
        left_ref[i, LANE:, :] = pays[i][size : 2 * size].T
    for i in range(leaves):

        def some(c, _, i=i):
            for t in [c * STEP + u for u in range(STEP)]:

                @pl.when((t > 0) & (t < cnt_ref[i]))
                def _(t=t):
                    load(i, t).wait()

            for t in [c * STEP + u for u in range(STEP)]:
                g = dot(left_ref[i], a_buf[i, t])
                g_s = g[:LANE]
                hi, lo = split2(g_s - g[LANE:])
                g_buf[i, t, 0] = hi
                g_buf[i, t, 1] = lo
                g_buf[i, t, 2] = g_s.astype(BF16)
            for t in [c * STEP + u for u in range(STEP)]:

                @pl.when((t > 0) & (t < cnt_ref[i]))
                def _(t=t):
                    save(i, t).start()

        lax.fori_loop(0, (cnt_ref[i] + (STEP - 1)) // STEP, some, None)
    for i in range(leaves):
        lax.fori_loop(1, cnt_ref[i], lambda t, _, i=i: save(i, t).wait(), None)


def own_part(counts, near_blocks, pays):
    leaves, slots, size, _ = near_blocks.shape
    shape = (leaves, slots, 3, LANE, size)
    return pl.pallas_call(
        own_kernel,
        in_specs=[SMEM, HBM] + [VMEM] * len(pays),
        out_specs=HBM,
        out_shape=jax.ShapeDtypeStruct(shape, BF16),
        scratch_shapes=[
            pltpu.VMEM(near_blocks.shape, BF16),
            pltpu.VMEM(shape, BF16),
            pltpu.VMEM((leaves, 2 * LANE, size), BF16),
            pltpu.SemaphoreType.DMA((leaves, slots)),
            pltpu.SemaphoreType.DMA((leaves, slots)),
        ],
        compiler_params=LARGE,
        cost_estimate=guess(8),
        name="own",
    )(counts, near_blocks, *pays)


def parent(first_ref, second_ref, far_ref, v_ref, factor_ref, top_ref, w_ref, t_ref):
    n = LANE
    row = lax.broadcasted_iota(jnp.int32, (n, n), 0)
    col = lax.broadcasted_iota(jnp.int32, (n, n), 1)
    far = far_ref[0]
    merged = jnp.concatenate(
        [
            jnp.concatenate([unpack_symmetric(first_ref[...]), far], axis=1),
            jnp.concatenate([far.T, unpack_symmetric(second_ref[...])], axis=1),
        ],
        axis=0,
    )
    v = v_ref[0]
    mh, ml = split2(merged)
    hh, hl = split2(dot(mh, v) + dot(ml, v))
    p = dot_first(v, hh) + dot_first(v, hl)
    w_ref[...] = p[:n, :n]
    lower_inverse([w_ref], [t_ref])
    x = mul3(t_ref[...], p[:n, n:])
    top_ref[0] = p[n:, n:] - mul3(x, x, dot_first)
    factor_ref[0] = jnp.where(row <= col, w_ref[...], 0.0).T


def near_kernel(off_ref, spot_ref, cnt_ref, schur_ref, g_hbm, first_ref, second_ref, far_ref, v_ref, *refs):
    pieces, (out_ref, factor_ref, top_ref, g_buf, r_buf, w_ref, t_ref, g_sem, r_sem) = refs[:-9], refs[-9:]
    leaves, slots = out_ref.shape[:2]
    rows = r_buf.shape[2]
    half = len(pieces) // 2
    count = pieces[0].shape[0]

    def load(i, t):
        return pltpu.make_async_copy(g_hbm.at[i, t], g_buf.at[i, t], g_sem.at[i, t])

    def fetch(i, t, piece, at):
        return pltpu.make_async_copy(piece.at[at, pl.ds(0, rows)], r_buf.at[i, t], r_sem.at[i, t])

    for i in range(leaves):

        def begin(t, _, i=i):
            load(i, t).start()
            at = i * slots + t
            spot = spot_ref[at]
            number = lax.rem(off_ref[at], 2) * half + lax.div(spot, count)
            for p, piece in enumerate(pieces):

                @pl.when(number == p)
                def _(piece=piece):
                    fetch(i, t, piece, lax.rem(spot, count)).start()

        lax.fori_loop(1, cnt_ref[i], begin, None)
    parent(first_ref, second_ref, far_ref, v_ref, factor_ref, top_ref, w_ref, t_ref)
    size = rows // 2
    for i in range(leaves):

        def some(c, _, i=i):
            for t in [c * STEP + u for u in range(STEP)]:

                @pl.when((t > 0) & (t < cnt_ref[i]))
                def _(t=t):
                    load(i, t).wait()
                    fetch(i, t, pieces[0], 0).wait()

            for t in [c * STEP + u for u in range(STEP)]:
                s_j = r_buf[i, t, :size]
                both = dot(g_buf[i, t, :2].reshape(2 * LANE, size), s_j)
                value = both[:LANE] + both[LANE:] - dot(g_buf[i, t, 2], r_buf[i, t, size:])
                out_ref[i, t] = jnp.where(t < cnt_ref[i], value, 0.0)

        def dead(t, _, i=i):
            out_ref[i, t] = jnp.zeros(out_ref.shape[2:], F32)

        steps = (cnt_ref[i] + (STEP - 1)) // STEP
        lax.fori_loop(0, steps, some, None)
        lax.fori_loop(steps * STEP, slots, dead, None)
        out_ref[i, 0] = schur_ref[i]


def near_part(offsets, spots, counts, schur, g, first, second, far, basis, pieces):
    leaves, slots, _, _, size = g.shape
    shape = jax.ShapeDtypeStruct((1, LANE, LANE), F32)
    return pl.pallas_call(
        near_kernel,
        in_specs=[SMEM, SMEM, SMEM, VMEM, HBM, VMEM, VMEM, VMEM, VMEM] + [HBM] * len(pieces),
        out_specs=[VMEM, VMEM, VMEM],
        out_shape=[jax.ShapeDtypeStruct((leaves, slots, LANE, LANE), F32), shape, shape],
        scratch_shapes=[
            pltpu.VMEM(g.shape, BF16),
            pltpu.VMEM((leaves, slots, 2 * size, LANE), BF16),
            pltpu.VMEM((LANE, LANE), F32),
            pltpu.VMEM((LANE, LANE), F32),
            pltpu.SemaphoreType.DMA((leaves, slots)),
            pltpu.SemaphoreType.DMA((leaves, slots)),
        ],
        compiler_params=LARGE,
        cost_estimate=guess(12),
        name="near",
    )(offsets, spots, counts, schur, g, first, second, far, basis, *pieces)


def shifted(x, side, step_z, step_x):
    route = []
    for i in range(side * side):
        z, w = divmod(i, side)
        route.append((i, (z + step_z) % side * side + (w + step_x) % side))
    return lax.ppermute(x, "col", route)


def ways(side):
    def along_x(v, d):
        return shifted(v, side, 0, d)

    def along_z(v, d):
        return shifted(v, side, d, 0)

    return along_x, along_z


def near_ring(x, shift):
    return shift(x, 1), shift(x, -1)


def place(delta):
    return jnp.where(delta == 0, 0, jnp.where(delta == 3, 1, jnp.where(delta == 1, 2, 3)))


def local(near_blocks, leaf_basis, near_cols, near_count, children, parent_basis, far_coupling):
    leaves, slots = near_cols.shape
    row_index = lax.axis_index("row")
    col_index = lax.axis_index("col")
    row_count = lax.axis_size("row")
    col_count = lax.axis_size("col")
    side = 4
    group_size = leaves * col_count
    group_base = row_index * group_size

    def spot(offset):
        device = offset // 2
        z = place((device // side - col_index // side) % side)
        x = place((device % side - col_index % side) % side)
        return jnp.where(offset % 2 == 0, z * side + x, x * side + z)

    partner_row = row_index + 1 - 2 * (row_index % 2)
    parent_id = row_index * col_count + col_index
    partner_parent = partner_row * col_count + col_index
    child = jnp.stack([children[parent_id, 0], children[partner_parent, 1]]) - group_base
    where = jnp.stack([child % 2, spot(child)], axis=1).reshape(-1)
    offsets = (near_cols - group_base).reshape(-1)
    spots = spot(offsets)

    hold = lax.optimization_barrier
    first_way, second_way = ways(side)
    orders = ((first_way, second_way), (second_way, first_way))
    factors, schur, *pays = diag_part(near_blocks, leaf_basis)
    near = [near_ring(pays[k], orders[k][0]) for k in range(2)]
    low = [jnp.stack([pays[k], near[k][0]]) for k in range(2)]
    low_far = [near_ring(low[k], orders[k][1]) for k in range(2)]
    far = [orders[0][0](near[0][0], 1), orders[1][0](near[1][1], -1)]
    own_pays, _ = hold((pays, low))
    g = own_part(near_count, near_blocks, own_pays)
    g, ahead, far = hold((g, [near[k][1] for k in range(2)], far))
    high = [jnp.stack([ahead[k], far[k]]) for k in range(2)]
    high_far = [near_ring(high[k], orders[k][1]) for k in range(2)]
    pieces = []
    for k in range(2):
        shift = orders[k][1]
        pieces += [low[k], high[k], low_far[k][0], high_far[k][0], low_far[k][1], high_far[k][1]]
        pieces += [shift(low_far[k][0], 1), shift(high_far[k][1], -1)]
    first, outgoing = pick_part(where, pieces)
    second = lax.ppermute(outgoing, "row", [(r, r ^ 1) for r in range(row_count)])
    near_schur, top_factor, top_schur = near_part(
        offsets, spots, near_count, schur, g, first, second, far_coupling, parent_basis, pieces
    )
    return factors, near_schur, top_factor, top_schur


def solution(mesh):
    both = ("row", "col")
    return jax.shard_map(
        local,
        mesh=mesh,
        in_specs=(P(both), P(both), P(both), P(both), P(), P(both), P(both)),
        out_specs=(P(both), P(both), P(both), P(both)),
        check_vma=False,
    )
```
